32 devices in a mesh: gy: 4 (over z), gx: 8 (over y, x, core).
Axes of the slice: x: 2, y: 2, z: 4, core: 2. Of those that a mesh axis runs over, the one named last changes fastest.
Arguments:
- tiles: bfloat16 [4096, 128, 128], P(('gy', 'gx')), may hold values from 0.19921875 to 5
- tile_dest: int32 [4096, 1], P(('gy', 'gx')), may hold values from 0 to 31, as said below
- tile_slot: int32 [4096], P(('gy', 'gx')), may hold values from 0 to 191
- psf: float32 [6, 3, 31], replicated, may hold values from 0.05 to 1
- estimate: float32 [32, 512, 1024], P(None, 'gy', 'gx'), may hold values from 0.5 to 2
Outputs:
- restored: float32 [32, 512, 1024], P(None, 'gy', 'gx')
The draws below stay inside these ranges and needn't reach their ends.
Inputs may be any that keep to these rules, and one draw needn't show every extreme that they name: `tile_dest`: among the 128 tiles held by one device no brick is named more than 8 times; in every draw some brick is named exactly 8 times by the tiles of every device.
All inputs are finite; a program needn't handle non-finite values.
Results may differ from the reference program's by a relative error of at most 0.00069.
Values may be sent and summed in bfloat16 or wider, within the bound.
A program may use at most 192 MiB of HBM per device.

```python
import math
import jax
import jax.numpy as jnp
from jax import lax

TILE = 128
CZ = 32
VIEWS = 6
TAPS = 31
ITERS = 2
TILES_DEV = 128
HALF = 15
SLOTS = 8
TILES = 4096
NY = 512
NX = 1024
N_GY = 4
N_GX = 8
DEVICES = 32


def draw_tile_dest(key, part):
    hottest = jax.random.randint(jax.random.fold_in(key, 7), (), 0, DEVICES)

    def holder(holder_index):
        holder_key = jax.random.fold_in(key, holder_index + 100)
        increments = jax.random.randint(jax.random.fold_in(holder_key, 1), (TILES_DEV - SLOTS,), 1, 3)
        position = jnp.cumsum(increments) - increments
        grouping = position // SLOTS
        ordering = jax.random.permutation(jax.random.fold_in(holder_key, 2), DEVICES - 1)
        picked = ordering[grouping]
        picked = picked + (picked >= hottest).astype(jnp.int32)
        return jnp.concatenate([jnp.full((SLOTS,), hottest, jnp.int32), picked.astype(jnp.int32)])
    targets = jax.vmap(holder)(jnp.arange(DEVICES))
    return targets.reshape(DEVICES * TILES_DEV, 1).astype(jnp.int32)


def with_ends(drawn, own_key, least, largest):
    longest = drawn.shape.index(max(drawn.shape))
    spots = []
    for shift in (0, 1):
        where = [jax.random.randint(jax.random.fold_in(own_key, axis), (), 0, length) for axis, length in enumerate(drawn.shape)]
        where[longest] = (where[longest] + shift) % drawn.shape[longest]
        spots.append(tuple(where))
    return drawn.at[spots[0]].set(least).at[spots[1]].set(largest)


def block_scale(rng, dims, cuts, least, high):
    def one(dim, parts):
        draws = jax.random.uniform(jax.random.fold_in(jax.random.fold_in(rng, 6), dim), (parts,), jnp.float32, least / len(cuts), high / len(cuts))
        return jnp.repeat(jnp.exp(draws), dims[dim] // parts).reshape((-1,) + (1,) * (len(dims) - dim - 1))

    gain = one(*cuts[0])
    for cut in cuts[1:]:
        gain = gain * one(*cut)
    return gain


def setup_inputs(seed: int = 0) -> dict:
    seeds = jax.random.split(jax.random.key(seed), 6)
    return {
        "tiles": jnp.clip(jnp.exp(math.log(5.0) - 3.2227897 * jax.random.uniform(seeds[0], (TILES, TILE, TILE), jnp.float32) ** block_scale(seeds[0], (TILES, TILE, TILE), ((0, 32),), -0.2, 0.2)), 0.19921875, 5.0).astype(jnp.bfloat16),
        "tile_dest": draw_tile_dest(jax.random.fold_in(seeds[5], 71), 0),
        "tile_slot": with_ends(jax.random.randint(seeds[2], (TILES,), 0, VIEWS * CZ), jax.random.fold_in(seeds[2], 1), 0, (VIEWS * CZ) - 1).astype(jnp.int32),
        "psf": jnp.clip(jnp.exp(jax.random.uniform(seeds[3], (VIEWS, 3, TAPS), jnp.float32, math.log(0.05), math.log(1.0))), 0.05, 1.0),
        "estimate": jnp.clip(jnp.exp(math.log(2.0) - 1.3862944 * jax.random.uniform(seeds[4], (CZ, NY, NX), jnp.float32) ** block_scale(seeds[4], (CZ, NY, NX), ((1, 4), (2, 8)), -0.2, 0.2)), 0.5, 2.0),
    }


damping = 0.05


def to_bf16(values):
    held = lax.optimization_barrier(values.astype(jnp.bfloat16))
    return held.astype(jnp.float32)


def conv_axis(volume, taps, axis):
    moved = jnp.moveaxis(volume, axis, -1)
    moved_shape = moved.shape
    rows_flat = moved.reshape(-1, 1, moved_shape[-1])
    filtered = lax.conv_general_dilated(rows_flat, taps.reshape(1, 1, -1), (1,), [(HALF, HALF)], precision=lax.Precision.HIGHEST)
    return jnp.moveaxis(filtered.reshape(moved_shape), -1, axis)


def observe(tiles_flat, target, tile_slot, view_index):
    bricks = N_GY * N_GX
    segment_ids = jnp.where(tile_slot // CZ == view_index, (tile_slot % CZ) * bricks + target, CZ * bricks).astype(jnp.int32)
    observed = jax.ops.segment_sum(tiles_flat, segment_ids, CZ * bricks + 1)[:-1]
    counted = jax.ops.segment_sum(jnp.ones(segment_ids.shape, jnp.float32), segment_ids, CZ * bricks + 1)[:-1]
    observed = observed.reshape(CZ, N_GY, N_GX, TILE, TILE).transpose(0, 1, 3, 2, 4).reshape(CZ, NY, NX)
    return observed, counted.reshape(CZ, N_GY, N_GX)


def reference(tiles, tile_dest, tile_slot, psf, estimate):
    kernel = (psf / jnp.sum(psf, axis=2, keepdims=True)).astype(jnp.bfloat16).astype(jnp.float32)
    flipped = kernel[:, :, ::-1]
    target = tile_dest[:, 0]
    tiles_flat = tiles.astype(jnp.float32).reshape(-1, TILE * TILE)
    for repeat_index in range(ITERS):
        rounded = to_bf16(estimate)
        total = jnp.zeros(estimate.shape, jnp.float32)
        for view_index in range(VIEWS):
            along_x = to_bf16(conv_axis(rounded, kernel[view_index, 2], 2))
            along_y = to_bf16(conv_axis(along_x, kernel[view_index, 1], 1))
            blur = conv_axis(along_y, kernel[view_index, 0], 0)
            observed, counted = observe(tiles_flat, target, tile_slot, view_index)
            scaled = blur.reshape(CZ, N_GY, TILE, N_GX, TILE) * counted[:, :, None, :, None]
            ratio = to_bf16((observed + damping) / (scaled.reshape(CZ, NY, NX) + damping))
            back_z = to_bf16(conv_axis(ratio, flipped[view_index, 0], 0))
            back_y = to_bf16(conv_axis(back_z, flipped[view_index, 1], 1))
            total = total + conv_axis(back_y, flipped[view_index, 2], 2)
        estimate = estimate * total / VIEWS
    return estimate
```

```python
import functools

import jax
import jax.numpy as jnp
from jax import lax
from jax.experimental import pallas as pl
from jax.experimental.pallas import tpu as pltpu
from jax.sharding import PartitionSpec as P

ITERS = 2
PAD = 16
VMEM = 56 * 1024 * 1024

damping = 0.05


def coordinate(index, side):
    return jnp.where(index < side, index, jnp.where(index < side + PAD, index - side - PAD, index - PAD))


def toeplitz(taps_ref, row, offset):
    def add(t, held):
        return jnp.where(offset == t, taps_ref[row, t], held)

    return lax.fori_loop(0, taps_ref.shape[1], add, jnp.zeros(offset.shape, jnp.float32))


def bands_kernel(reach, planes, side, taps_ref, bx_ref, by_ref, kz_ref, kf_ref, fy_ref, fx_ref):
    views = by_ref.shape[0]
    ext = side + 2 * PAD
    wide = fx_ref.shape[1]
    iota = lambda shape, dim: lax.broadcasted_iota(jnp.int32, shape, dim)
    tall_off = coordinate(iota((ext, side), 0), side) - iota((ext, side), 1) + reach
    long_ext = iota((side, wide), 1)
    long_off = coordinate(long_ext, side) - iota((side, wide), 0) + reach
    long_off = jnp.where(long_ext < ext, long_off, -1)
    lanes = 128
    z_col = iota((planes, lanes), 1)
    z_diff = z_col - iota((planes, lanes), 0)
    full = planes * 8
    spread_l = (iota((full, planes), 0) // 8 == iota((full, planes), 1)).astype(jnp.bfloat16)
    spread_r = (iota((lanes, full), 1) // 8 == iota((lanes, full), 0)).astype(jnp.bfloat16)
    same = iota((full, full), 0) % 8 == iota((full, full), 1) % 8

    def kron(row, offset):
        small = toeplitz(taps_ref, row, offset).astype(jnp.bfloat16)
        right = jnp.dot(small, spread_r, preferred_element_type=jnp.float32).astype(jnp.bfloat16)
        both = jnp.dot(spread_l, right, preferred_element_type=jnp.float32)
        return jnp.where(same, both, 0.0).astype(jnp.bfloat16)

    for v in range(views):
        kz_ref[v] = kron(3 * v, jnp.where(z_col < planes, z_diff + reach, -1))
        kf_ref[v] = kron(3 * v, jnp.where(z_col < planes, reach - z_diff, -1))
        tall_y = toeplitz(taps_ref, 3 * v + 1, tall_off)
        long_y = toeplitz(taps_ref, 3 * v + 1, long_off)
        fy_ref[v] = tall_y.astype(jnp.bfloat16)
        by_ref[v] = long_y[:, :ext].astype(jnp.bfloat16)
        tall_x = toeplitz(taps_ref, 3 * v + 2, tall_off)
        long_x = toeplitz(taps_ref, 3 * v + 2, long_off)
        bx_ref[:, v * side : (v + 1) * side] = tall_x.astype(jnp.bfloat16)
        fx_ref[v * side : (v + 1) * side, :] = long_x.astype(jnp.bfloat16)


def bands(taps, planes, side):
    views = taps.shape[0] // 3
    ext = side + 2 * PAD
    shapes = [
        (ext, views * side),
        (views, side, ext),
        (views, planes * 8, planes * 8),
        (views, planes * 8, planes * 8),
        (views, ext, side),
        (views * side, 2 * side),
    ]
    return pl.pallas_call(
        functools.partial(bands_kernel, (taps.shape[1] - 1) // 2, planes, side),
        out_shape=[jax.ShapeDtypeStruct(s, jnp.bfloat16) for s in shapes],
        in_specs=[pl.BlockSpec(memory_space=pltpu.SMEM)],
        out_specs=[pl.BlockSpec(memory_space=pltpu.VMEM)] * len(shapes),
        compiler_params=pltpu.CompilerParams(vmem_limit_bytes=VMEM),
        name="bands",
    )(taps)


def pack_kernel(pick_ref, tiles_ref, out_ref, sem):
    count = out_ref.shape[0]

    def send(slot, carry):
        pltpu.make_async_copy(tiles_ref.at[pick_ref[slot]], out_ref.at[slot], sem).start()
        return carry

    lax.fori_loop(0, count, send, 0)
    pltpu.make_async_copy(out_ref, out_ref, sem).wait()


def pack(pick, tiles):
    count = pick.shape[0]
    return pl.pallas_call(
        pack_kernel,
        out_shape=jax.ShapeDtypeStruct((count,) + tiles.shape[1:], tiles.dtype),
        in_specs=[pl.BlockSpec(memory_space=pltpu.SMEM), pl.BlockSpec(memory_space=pltpu.VMEM)],
        out_specs=pl.BlockSpec(memory_space=pl.ANY),
        scratch_shapes=[pltpu.SemaphoreType.DMA],
        compiler_params=pltpu.CompilerParams(vmem_limit_bytes=VMEM),
        name="pack",
    )(pick, tiles)


def observe_kernel(chunk, label_ref, tiles_ref, out_ref):
    step = pl.program_id(0)

    @pl.when(step == 0)
    def _():
        def clear(plane, carry):
            out_ref[plane] = jnp.zeros(out_ref.shape[1:], out_ref.dtype)
            return carry

        lax.fori_loop(0, out_ref.shape[0], clear, 0)

    def add(i, carry):
        label = label_ref[step * chunk + i]

        @pl.when(label >= 0)
        def _():
            out_ref[label] += tiles_ref[i].astype(jnp.float32)

        return carry

    lax.fori_loop(0, chunk, add, 0)


def observe(labels, tiles, slots):
    chunk = 32
    side = tiles.shape[1]
    return pl.pallas_call(
        functools.partial(observe_kernel, chunk),
        out_shape=jax.ShapeDtypeStruct((slots, side, side), jnp.float32),
        grid=(tiles.shape[0] // chunk,),
        in_specs=[
            pl.BlockSpec(memory_space=pltpu.SMEM),
            pl.BlockSpec((chunk, side, side), lambda i: (i, 0, 0)),
        ],
        out_specs=pl.BlockSpec((slots, side, side), lambda i: (0, 0, 0)),
        compiler_params=pltpu.CompilerParams(vmem_limit_bytes=VMEM),
        name="observe",
    )(labels, tiles)


def sides_kernel(wide_ref, bx_ref, by_ref, out_ref):
    views, planes, side, _ = out_ref.shape
    for z in range(planes):
        along_x = jnp.dot(wide_ref[z], bx_ref[...], preferred_element_type=jnp.float32).astype(jnp.bfloat16)
        for v in range(views):
            out_ref[v, z] = jnp.dot(
                by_ref[v], along_x[:, v * side : (v + 1) * side], preferred_element_type=jnp.float32
            ).astype(jnp.bfloat16)


def sides(wide, bx, by):
    planes, ext, _ = wide.shape
    views, side, _ = by.shape
    chunk = 4
    macs = planes * ext * ext * side * views + planes * views * side * side * ext
    return pl.pallas_call(
        sides_kernel,
        out_shape=jax.ShapeDtypeStruct((views, planes, side, side), jnp.bfloat16),
        grid=(planes // chunk,),
        in_specs=[
            pl.BlockSpec((chunk, ext, ext), lambda i: (i, 0, 0)),
            pl.BlockSpec(bx.shape, lambda i: (0, 0)),
            pl.BlockSpec(by.shape, lambda i: (0, 0, 0)),
        ],
        out_specs=pl.BlockSpec((views, chunk, side, side), lambda i: (0, i, 0, 0)),
        compiler_params=pltpu.CompilerParams(vmem_limit_bytes=VMEM),
        cost_estimate=pl.CostEstimate(flops=2 * macs, bytes_accessed=views * planes * side * side * 3, transcendentals=0),
        name="sides",
    )(wide, bx, by)


def depth_kernel(sides_ref, seen_ref, count_ref, kz_ref, kf_ref, out_ref):
    _, planes, rows, side = sides_ref.shape
    full = planes * 8
    pairs = rows // 16
    count = jnp.broadcast_to(count_ref[0][:, None, :], (planes, 8, side)).reshape(full, side)
    count = jnp.concatenate([count, count], axis=1)

    def both(values):
        return jnp.concatenate([values[:, :8].reshape(full, side), values[:, 8:].reshape(full, side)], axis=1)

    for p in range(pairs):
        spot = slice(p * 16, p * 16 + 16)
        stack = both(sides_ref[0, :, spot].astype(jnp.float32)).astype(jnp.bfloat16)
        blur = jnp.dot(kz_ref[0], stack, preferred_element_type=jnp.float32)
        seen = both(seen_ref[0, :, spot].astype(jnp.float32))
        ratio = ((seen + damping) / (count * blur + damping)).astype(jnp.bfloat16)
        back = jnp.dot(kf_ref[0], ratio, preferred_element_type=jnp.float32)
        out_ref[0, :, spot] = jnp.concatenate(
            [back[:, :side].reshape(planes, 8, side), back[:, side:].reshape(planes, 8, side)], axis=1
        ).astype(jnp.bfloat16)


def depth(along, seen, count, kz, kf):
    views, planes, side, _ = along.shape
    rows = 128
    block = pl.BlockSpec((1, planes, rows, side), lambda v, i: (v, 0, i, 0))
    per_view = lambda a: pl.BlockSpec((1,) + a.shape[1:], lambda v, i: (v,) + (0,) * (a.ndim - 1))
    return pl.pallas_call(
        depth_kernel,
        out_shape=jax.ShapeDtypeStruct(along.shape, jnp.bfloat16),
        grid=(views, side // rows),
        in_specs=[block, block, per_view(count), per_view(kz), per_view(kf)],
        out_specs=block,
        compiler_params=pltpu.CompilerParams(vmem_limit_bytes=VMEM),
        name="depth",
    )(along, seen, count, kz, kf)


def spread_kernel(back_ref, fy_ref, fx_ref, out_ref):
    views, planes, _, _ = back_ref.shape
    for z in range(planes):
        wide = jnp.concatenate(
            [
                jnp.dot(fy_ref[v], back_ref[v, z], preferred_element_type=jnp.float32).astype(jnp.bfloat16)
                for v in range(views)
            ],
            axis=1,
        )
        out_ref[z] = jnp.dot(wide, fx_ref[...], preferred_element_type=jnp.float32)


def spread(back, fy, fx):
    views, planes, side, _ = back.shape
    ext = fy.shape[1]
    chunk = 4
    return pl.pallas_call(
        spread_kernel,
        out_shape=jax.ShapeDtypeStruct((planes, ext, fx.shape[1]), jnp.float32),
        grid=(planes // chunk,),
        in_specs=[
            pl.BlockSpec((views, chunk, side, side), lambda i: (0, i, 0, 0)),
            pl.BlockSpec(fy.shape, lambda i: (0, 0, 0)),
            pl.BlockSpec(fx.shape, lambda i: (0, 0)),
        ],
        out_specs=pl.BlockSpec((chunk, ext, fx.shape[1]), lambda i: (i, 0, 0)),
        compiler_params=pltpu.CompilerParams(vmem_limit_bytes=VMEM),
        name="spread",
    )(back, fy, fx)


def shift(values, axis, way):
    count = lax.axis_size(axis)
    pairs = [(i, i + 1) for i in range(count - 1)]
    return lax.ppermute(values, axis, pairs if way > 0 else [(b, a) for a, b in pairs])


def widened(estimate):
    cells = estimate.astype(jnp.bfloat16)
    for axis, dim in (("gy", 1), ("gx", 2)):
        side = cells.shape[dim]
        head = lax.slice_in_dim(cells, 0, PAD, axis=dim)
        tail = lax.slice_in_dim(cells, side - PAD, side, axis=dim)
        cells = jnp.concatenate([cells, shift(tail, axis, 1), shift(head, axis, -1)], axis=dim)
    return cells


def gathered(partial, side):
    ext = side + 2 * PAD
    total = partial
    for axis, dim in (("gy", 1), ("gx", 2)):
        before = lax.slice_in_dim(total, side, side + PAD, axis=dim).astype(jnp.bfloat16)
        after = lax.slice_in_dim(total, side + PAD, ext, axis=dim).astype(jnp.bfloat16)
        to_tail = shift(before, axis, -1).astype(jnp.float32)
        to_head = shift(after, axis, 1).astype(jnp.float32)
        inner = lax.slice_in_dim(total, 0, side, axis=dim)
        total = jnp.concatenate(
            [
                lax.slice_in_dim(inner, 0, PAD, axis=dim) + to_head,
                lax.slice_in_dim(inner, PAD, side - PAD, axis=dim),
                lax.slice_in_dim(inner, side - PAD, side, axis=dim) + to_tail,
            ],
            axis=dim,
        )
    return total


def local(tiles, tile_dest, tile_slot, psf, estimate):
    devices = lax.axis_size("gy") * lax.axis_size("gx")
    holding, side, _ = tiles.shape
    slot_count = 2 * ((holding + devices - 1) // devices)
    views, _, taps = psf.shape
    planes = estimate.shape[0]
    target = tile_dest[:, 0]
    earlier = (target[None, :] == target[:, None]) & (
        jnp.arange(holding)[None, :] < jnp.arange(holding)[:, None]
    )
    rank = jnp.sum(earlier.astype(jnp.int32), axis=1)
    where_to = target * slot_count + rank
    placing = where_to[None, :] == jnp.arange(devices * slot_count)[:, None]
    pick = jnp.sum(jnp.where(placing, jnp.arange(holding, dtype=jnp.int32)[None, :], 0), axis=1)
    labels = jnp.sum(jnp.where(placing, tile_slot[None, :] + 1, 0), axis=1) - 1
    packed = pack(pick, tiles)
    exchange = functools.partial(
        lax.all_to_all, axis_name=("gy", "gx"), split_axis=0, concat_axis=0, tiled=True
    )
    got_labels = exchange(labels.reshape(devices, slot_count)).reshape(-1)
    got_tiles = exchange(packed.reshape(devices, slot_count, side, side)).reshape(-1, side, side)

    kernel = (psf / jnp.sum(psf, axis=2, keepdims=True)).astype(jnp.bfloat16).astype(jnp.float32)
    bx, by, kz, kf, fy, fx = bands(kernel.reshape(views * 3, taps), planes, side)
    along = sides(widened(estimate), bx, by)

    seen = observe(got_labels, got_tiles, views * planes).reshape(views, planes, side, side)
    sorting = got_labels[None, :] == jnp.arange(views * planes)[:, None]
    counted = jnp.sum(sorting.astype(jnp.float32), axis=1).reshape(views, planes)
    count = jnp.broadcast_to(counted[:, :, None], (views, planes, side))
    for repeat_index in range(ITERS):
        if repeat_index:
            along = sides(widened(estimate), bx, by)
        back = depth(along, seen, count, kz, kf)
        estimate = estimate * gathered(spread(back, fy, fx), side) / views
    return estimate


def solution(mesh):
    placed = (
        P(("gy", "gx"), None, None),
        P(("gy", "gx"), None),
        P(("gy", "gx")),
        P(),
        P(None, "gy", "gx"),
    )
    return jax.shard_map(
        local, mesh=mesh, in_specs=placed, out_specs=P(None, "gy", "gx"), check_vma=False
    )
```

```python
import functools

import jax
import jax.numpy as jnp
from jax import lax
from jax.experimental import pallas as pl
from jax.experimental.pallas import tpu as pltpu
from jax.sharding import PartitionSpec as P

ITERS = 2
PAD = 16
VMEM = 56 * 1024 * 1024

damping = 0.05


def coordinate(index, side):
    return jnp.where(index < side, index, jnp.where(index < side + PAD, index - side - PAD, index - PAD))


def toeplitz(taps_ref, row, offset):
    def add(t, held):
        return jnp.where(offset == t, taps_ref[row, t], held)

    return lax.fori_loop(0, taps_ref.shape[1], add, jnp.zeros(offset.shape, jnp.float32))


def bands_kernel(reach, planes, side, taps_ref, bx_ref, by_ref, kz_ref, kf_ref, fy_ref, fx_ref):
    views = by_ref.shape[0]
    ext = side + 2 * PAD
    wide = fx_ref.shape[1]
    iota = lambda shape, dim: lax.broadcasted_iota(jnp.int32, shape, dim)
    tall_off = coordinate(iota((ext, side), 0), side) - iota((ext, side), 1) + reach
    long_ext = iota((side, wide), 1)
    long_off = coordinate(long_ext, side) - iota((side, wide), 0) + reach
    long_off = jnp.where(long_ext < ext, long_off, -1)
    lanes = 128
    z_col = iota((planes, lanes), 1)
    z_diff = z_col - iota((planes, lanes), 0)
    full = planes * 8
    spread_l = (iota((full, planes), 0) // 8 == iota((full, planes), 1)).astype(jnp.bfloat16)
    spread_r = (iota((lanes, full), 1) // 8 == iota((lanes, full), 0)).astype(jnp.bfloat16)
    same = iota((full, full), 0) % 8 == iota((full, full), 1) % 8

    def kron(row, offset):
        small = toeplitz(taps_ref, row, offset).astype(jnp.bfloat16)
        right = jnp.dot(small, spread_r, preferred_element_type=jnp.float32).astype(jnp.bfloat16)
        both = jnp.dot(spread_l, right, preferred_element_type=jnp.float32)
        return jnp.where(same, both, 0.0).astype(jnp.bfloat16)

    for v in range(views):
        kz_ref[v] = kron(3 * v, jnp.where(z_col < planes, z_diff + reach, -1))
        kf_ref[v] = kron(3 * v, jnp.where(z_col < planes, reach - z_diff, -1))
        tall_y = toeplitz(taps_ref, 3 * v + 1, tall_off)
        long_y = toeplitz(taps_ref, 3 * v + 1, long_off)
        fy_ref[v] = tall_y.astype(jnp.bfloat16)
        by_ref[v] = long_y[:, :ext].astype(jnp.bfloat16)
        tall_x = toeplitz(taps_ref, 3 * v + 2, tall_off)
        long_x = toeplitz(taps_ref, 3 * v + 2, long_off)
        bx_ref[:ext, v * side : (v + 1) * side] = tall_x.astype(jnp.bfloat16)
        bx_ref[ext:, v * side : (v + 1) * side] = jnp.zeros((wide - ext, side), jnp.bfloat16)
        fx_ref[v * side : (v + 1) * side, :] = long_x.astype(jnp.bfloat16)


def bands(taps, planes, side):
    views = taps.shape[0] // 3
    ext = side + 2 * PAD
    shapes = [
        (2 * side, views * side),
        (views, side, ext),
        (views, planes * 8, planes * 8),
        (views, planes * 8, planes * 8),
        (views, ext, side),
        (views * side, 2 * side),
    ]
    return pl.pallas_call(
        functools.partial(bands_kernel, (taps.shape[1] - 1) // 2, planes, side),
        out_shape=[jax.ShapeDtypeStruct(s, jnp.bfloat16) for s in shapes],
        in_specs=[pl.BlockSpec(memory_space=pltpu.SMEM)],
        out_specs=[pl.BlockSpec(memory_space=pltpu.VMEM)] * len(shapes),
        compiler_params=pltpu.CompilerParams(vmem_limit_bytes=VMEM),
        name="bands",
    )(taps)


def pack_kernel(pick_ref, tiles_ref, out_ref, sem):
    count = out_ref.shape[0]

    def send(slot, carry):
        pltpu.make_async_copy(tiles_ref.at[pick_ref[slot]], out_ref.at[slot], sem).start()
        return carry

    lax.fori_loop(0, count, send, 0)
    pltpu.make_async_copy(out_ref, out_ref, sem).wait()


def pack(pick, tiles):
    count = pick.shape[0]
    return pl.pallas_call(
        pack_kernel,
        out_shape=jax.ShapeDtypeStruct((count,) + tiles.shape[1:], tiles.dtype),
        in_specs=[pl.BlockSpec(memory_space=pltpu.SMEM), pl.BlockSpec(memory_space=pltpu.VMEM)],
        out_specs=pl.BlockSpec(memory_space=pl.ANY),
        scratch_shapes=[pltpu.SemaphoreType.DMA],
        compiler_params=pltpu.CompilerParams(vmem_limit_bytes=VMEM),
        name="pack",
    )(pick, tiles)


def observe_kernel(chunk, label_ref, tiles_ref, out_ref):
    step = pl.program_id(0)

    @pl.when(step == 0)
    def _():
        def clear(plane, carry):
            out_ref[plane] = jnp.zeros(out_ref.shape[1:], out_ref.dtype)
            return carry

        lax.fori_loop(0, out_ref.shape[0], clear, 0)

    def add(i, carry):
        label = label_ref[step * chunk + i]

        @pl.when(label >= 0)
        def _():
            out_ref[label] += tiles_ref[i].astype(jnp.float32)

        return carry

    lax.fori_loop(0, chunk, add, 0)


def observe(labels, tiles, slots):
    chunk = 32
    side = tiles.shape[1]
    return pl.pallas_call(
        functools.partial(observe_kernel, chunk),
        out_shape=jax.ShapeDtypeStruct((slots, side, side), jnp.float32),
        grid=(tiles.shape[0] // chunk,),
        in_specs=[
            pl.BlockSpec(memory_space=pltpu.SMEM),
            pl.BlockSpec((chunk, side, side), lambda i: (i, 0, 0)),
        ],
        out_specs=pl.BlockSpec((slots, side, side), lambda i: (0, 0, 0)),
        compiler_params=pltpu.CompilerParams(vmem_limit_bytes=VMEM),
        name="observe",
    )(labels, tiles)


def sides_kernel(wide_ref, bx_ref, by_ref, out_ref):
    views, planes, side, _ = out_ref.shape
    for z in range(planes):
        along_x = jnp.dot(wide_ref[z], bx_ref[...], preferred_element_type=jnp.float32).astype(jnp.bfloat16)
        for v in range(views):
            out_ref[v, z] = jnp.dot(
                by_ref[v], along_x[:, v * side : (v + 1) * side], preferred_element_type=jnp.float32
            ).astype(jnp.bfloat16)


def sides(wide, bx, by):
    planes, ext, _ = wide.shape
    views, side, _ = by.shape
    chunk = 4
    macs = planes * ext * ext * side * views + planes * views * side * side * ext
    return pl.pallas_call(
        sides_kernel,
        out_shape=jax.ShapeDtypeStruct((views, planes, side, side), jnp.bfloat16),
        grid=(planes // chunk,),
        in_specs=[
            pl.BlockSpec((chunk,) + wide.shape[1:], lambda i: (i, 0, 0)),
            pl.BlockSpec(bx.shape, lambda i: (0, 0)),
            pl.BlockSpec(by.shape, lambda i: (0, 0, 0)),
        ],
        out_specs=pl.BlockSpec((views, chunk, side, side), lambda i: (0, i, 0, 0)),
        compiler_params=pltpu.CompilerParams(vmem_limit_bytes=VMEM),
        cost_estimate=pl.CostEstimate(flops=2 * macs, bytes_accessed=views * planes * side * side * 3, transcendentals=0),
        name="sides",
    )(wide, bx, by)


def depth_kernel(sides_ref, seen_ref, count_ref, kz_ref, kf_ref, out_ref):
    _, planes, rows, side = sides_ref.shape
    full = planes * 8
    pairs = rows // 16
    count = jnp.broadcast_to(count_ref[0][:, None, :], (planes, 8, side)).reshape(full, side)
    count = jnp.concatenate([count, count], axis=1)

    def both(values):
        return jnp.concatenate([values[:, :8].reshape(full, side), values[:, 8:].reshape(full, side)], axis=1)

    for p in range(pairs):
        spot = slice(p * 16, p * 16 + 16)
        stack = both(sides_ref[0, :, spot].astype(jnp.float32)).astype(jnp.bfloat16)
        blur = jnp.dot(kz_ref[0], stack, preferred_element_type=jnp.float32)
        seen = both(seen_ref[0, :, spot].astype(jnp.float32))
        ratio = ((seen + damping) / (count * blur + damping)).astype(jnp.bfloat16)
        back = jnp.dot(kf_ref[0], ratio, preferred_element_type=jnp.float32)
        out_ref[0, :, spot] = jnp.concatenate(
            [back[:, :side].reshape(planes, 8, side), back[:, side:].reshape(planes, 8, side)], axis=1
        ).astype(jnp.bfloat16)


def depth(along, seen, count, kz, kf):
    views, planes, side, _ = along.shape
    rows = 128
    block = pl.BlockSpec((1, planes, rows, side), lambda v, i: (v, 0, i, 0))
    per_view = lambda a: pl.BlockSpec((1,) + a.shape[1:], lambda v, i: (v,) + (0,) * (a.ndim - 1))
    return pl.pallas_call(
        depth_kernel,
        out_shape=jax.ShapeDtypeStruct(along.shape, jnp.bfloat16),
        grid=(views, side // rows),
        in_specs=[block, block, per_view(count), per_view(kz), per_view(kf)],
        out_specs=block,
        compiler_params=pltpu.CompilerParams(vmem_limit_bytes=VMEM),
        name="depth",
    )(along, seen, count, kz, kf)


def fold_lanes(values, start):
    lane = lax.broadcasted_iota(jnp.int32, values[0].shape, 1)
    held = jnp.zeros(values[0].shape, jnp.float32)
    for k, one in enumerate(values):
        held = jnp.where(lane // PAD == k, pltpu.roll(one, (PAD * k - start) % 128, 1), held)
    return held


def unfold_lanes(held, k, start):
    lane = lax.broadcasted_iota(jnp.int32, held.shape, 1)
    return jnp.where(lane // PAD == start // PAD, pltpu.roll(held, (start - PAD * k) % 128, 1), 0.0)


def spread_kernel(back_ref, fy_ref, fx_ref, in_ref, ys_ref, xl_ref, xr_ref):
    views, planes, side, _ = back_ref.shape
    rims = []
    for z in range(planes):
        wide = jnp.concatenate(
            [
                jnp.dot(fy_ref[v], back_ref[v, z], preferred_element_type=jnp.float32).astype(jnp.bfloat16)
                for v in range(views)
            ],
            axis=1,
        )
        part = jnp.dot(wide, fx_ref[...], preferred_element_type=jnp.float32)
        in_ref[z] = part[:side, :side]
        ys_ref[z] = part[side:, :side].astype(jnp.bfloat16)
        rims.append(part[:, side:])
    xl_ref[0] = fold_lanes(rims, 0).astype(jnp.bfloat16)
    xr_ref[0] = fold_lanes(rims, PAD).astype(jnp.bfloat16)


def spread(back, fy, fx):
    views, planes, side, _ = back.shape
    ext = fy.shape[1]
    chunk = 8
    folds = planes // chunk
    fold = pl.BlockSpec((1, ext, side), lambda i: (i, 0, 0))
    return pl.pallas_call(
        spread_kernel,
        out_shape=[
            jax.ShapeDtypeStruct((planes, side, side), jnp.float32),
            jax.ShapeDtypeStruct((planes, 2 * PAD, side), jnp.bfloat16),
            jax.ShapeDtypeStruct((folds, ext, side), jnp.bfloat16),
            jax.ShapeDtypeStruct((folds, ext, side), jnp.bfloat16),
        ],
        grid=(folds,),
        in_specs=[
            pl.BlockSpec((views, chunk, side, side), lambda i: (0, i, 0, 0)),
            pl.BlockSpec(fy.shape, lambda i: (0, 0, 0)),
            pl.BlockSpec(fx.shape, lambda i: (0, 0)),
        ],
        out_specs=[
            pl.BlockSpec((chunk, side, side), lambda i: (i, 0, 0)),
            pl.BlockSpec((chunk, 2 * PAD, side), lambda i: (i, 0, 0)),
            fold,
            fold,
        ],
        compiler_params=pltpu.CompilerParams(vmem_limit_bytes=VMEM),
        name="spread",
    )(back, fy, fx)


NEAR = [(-1, 0), (1, 0), (0, -1), (0, 1), (-1, -1), (1, -1), (-1, 1), (1, 1)]


def inside(grid, dy, dx):
    ny, nx = grid
    y = lax.axis_index("gy") + dy
    x = lax.axis_index("gx") + dx
    return (y >= 0) & (y < ny) & (x >= 0) & (x < nx), (y, x)


def greet(grid):
    barrier = pltpu.get_barrier_semaphore()
    for dy, dx in NEAR:
        there, where = inside(grid, dy, dx)

        @pl.when(there)
        def _():
            pl.semaphore_signal(barrier, inc=1, device_id=where, device_id_type=pl.DeviceIdType.MESH)

    ny, nx = grid
    y, x = lax.axis_index("gy"), lax.axis_index("gx")
    tall = 3 - (y == 0).astype(jnp.int32) - (y == ny - 1).astype(jnp.int32)
    broad = 3 - (x == 0).astype(jnp.int32) - (x == nx - 1).astype(jnp.int32)
    pl.semaphore_wait(barrier, tall * broad - 1)


def swap(grid, moves, send_sems, recv_sems):
    def copy(i, where):
        source, dest = moves[i]
        return pltpu.make_async_remote_copy(
            src_ref=source, dst_ref=dest, send_sem=send_sems.at[i], recv_sem=recv_sems.at[i],
            device_id=where, device_id_type=pl.DeviceIdType.MESH,
        )

    for i, (dy, dx) in enumerate(NEAR):
        there, where = inside(grid, dy, dx)

        @pl.when(there)
        def _():
            copy(i, where).start()

    for i, (dy, dx) in enumerate(NEAR):
        there, where = inside(grid, -dy, -dx)

        @pl.when(there)
        def _():
            copy(i, where).wait_recv()

        @pl.when(jnp.logical_not(there))
        def _():
            dest = moves[i][1]
            dest[...] = jnp.zeros(dest.shape, dest.dtype)

    for i, (dy, dx) in enumerate(NEAR):
        there, where = inside(grid, dy, dx)

        @pl.when(there)
        def _():
            copy(i, where).wait_send()


def widen(grid, fresh, wide_ref, left, right, rows, from_left, from_right, send_sems, recv_sems):
    planes, ext, _ = wide_ref.shape
    side = ext - 2 * PAD

    def cut(p, carry):
        values = []
        for k in range(8):
            plane = fresh(p * 8 + k)
            values.append(plane)
            wide_ref[p * 8 + k, :side, :side] = plane.astype(jnp.bfloat16)
        left[p] = fold_lanes(values, 0).astype(jnp.bfloat16)
        right[p] = fold_lanes(values, side - PAD).astype(jnp.bfloat16)
        return carry

    lax.fori_loop(0, planes // 8, cut, 0)
    first, last = pl.ds(0, PAD), pl.ds(side - PAD, PAD)
    whole, before, after = pl.ds(0, side), pl.ds(side, PAD), pl.ds(side + PAD, PAD)
    lanes = pl.ds(0, side)
    moves = [
        (wide_ref.at[:, first, lanes], rows.at[:, pl.ds(PAD, PAD)]),
        (wide_ref.at[:, last, lanes], rows.at[:, pl.ds(0, PAD)]),
        (left, from_right.at[:, whole]),
        (right, from_left.at[:, whole]),
        (left.at[:, first], from_right.at[:, after]),
        (left.at[:, last], from_right.at[:, before]),
        (right.at[:, first], from_left.at[:, after]),
        (right.at[:, last], from_left.at[:, before]),
    ]
    swap(grid, moves, send_sems, recv_sems)

    def paste(p, carry):
        low = from_left[p].astype(jnp.float32)
        high = from_right[p].astype(jnp.float32)
        for k in range(8):
            rim = unfold_lanes(low, k, 0) + unfold_lanes(high, k, PAD)
            wide_ref[p * 8 + k, :, side:] = rim.astype(jnp.bfloat16)
            wide_ref[p * 8 + k, side:, :side] = rows[p * 8 + k]
        return carry

    lax.fori_loop(0, planes // 8, paste, 0)


def rim_scratch(planes, side):
    ext = side + 2 * PAD
    return [
        pltpu.VMEM((planes, 2 * PAD, side), jnp.bfloat16),
        pltpu.VMEM((planes // 8, ext, side), jnp.bfloat16),
        pltpu.VMEM((planes // 8, ext, side), jnp.bfloat16),
        pltpu.SemaphoreType.DMA((8,)),
        pltpu.SemaphoreType.DMA((8,)),
    ]


def fold_scratch(planes, side):
    return [pltpu.VMEM((planes // 8, side, side), jnp.bfloat16)] * 2


def gather(grid, in_ref, ys_ref, xl_ref, xr_ref, rows, from_left, from_right, send_sems, recv_sems):
    planes, side, _ = in_ref.shape
    whole, before, after = pl.ds(0, side), pl.ds(side, PAD), pl.ds(side + PAD, PAD)
    first, second = pl.ds(0, PAD), pl.ds(PAD, PAD)
    moves = [
        (ys_ref.at[:, first], rows.at[:, second]),
        (ys_ref.at[:, second], rows.at[:, first]),
        (xl_ref.at[:, whole], from_right.at[:, whole]),
        (xr_ref.at[:, whole], from_left.at[:, whole]),
        (xl_ref.at[:, before], from_right.at[:, after]),
        (xl_ref.at[:, after], from_right.at[:, before]),
        (xr_ref.at[:, before], from_left.at[:, after]),
        (xr_ref.at[:, after], from_left.at[:, before]),
    ]
    swap(grid, moves, send_sems, recv_sems)


def totals(z, p, k, in_ref, rows, from_left, from_right):
    side = in_ref.shape[1]
    gap = jnp.zeros((side - 2 * PAD, side), jnp.float32)
    edge = rows[z].astype(jnp.float32)

    def rim(held, start):
        held = held.astype(jnp.float32)
        body = held[:side] + jnp.concatenate([held[side : side + PAD], gap, held[side + PAD :]], axis=0)
        return unfold_lanes(body, k, start)

    total = in_ref[z] + jnp.concatenate([edge[:PAD], gap, edge[PAD:]], axis=0)
    return total + rim(from_left[p], 0) + rim(from_right[p], side - PAD)


def first_kernel(grid, est_ref, wide_ref, left, right, *rim):
    greet(grid)
    widen(grid, lambda z: est_ref[z], wide_ref, left, right, *rim)


def between_kernel(grid, views, est_ref, in_ref, ys_ref, xl_ref, xr_ref, new_ref, wide_ref, *scratch):
    greet(grid)
    rim, (left, right), again = scratch[:5], scratch[5:7], scratch[7:]
    gather(grid, in_ref, ys_ref, xl_ref, xr_ref, *rim)

    def update(p, carry):
        for k in range(8):
            z = p * 8 + k
            new_ref[z] = est_ref[z] * totals(z, p, k, in_ref, *rim[:3]) / views
        return carry

    lax.fori_loop(0, est_ref.shape[0] // 8, update, 0)
    widen(grid, lambda z: new_ref[z], wide_ref, left, right, *again)


def last_kernel(grid, in_ref, ys_ref, xl_ref, xr_ref, out_ref, *rim):
    greet(grid)
    gather(grid, in_ref, ys_ref, xl_ref, xr_ref, *rim)

    def update(p, carry):
        for k in range(8):
            z = p * 8 + k
            out_ref[z] = totals(z, p, k, in_ref, *rim[:3])
        return carry

    lax.fori_loop(0, in_ref.shape[0] // 8, update, 0)


def rim_call(kernel, name, number, shapes, scratch, args):
    held = pl.BlockSpec(memory_space=pltpu.VMEM)
    return pl.pallas_call(
        kernel,
        out_shape=shapes,
        in_specs=[held] * len(args),
        out_specs=[held] * len(shapes),
        scratch_shapes=scratch,
        compiler_params=pltpu.CompilerParams(
            vmem_limit_bytes=VMEM, collective_id=number, has_side_effects=True
        ),
        name=name,
    )(*args)


def local(tiles, tile_dest, tile_slot, psf, estimate):
    devices = lax.axis_size("gy") * lax.axis_size("gx")
    holding, side, _ = tiles.shape
    slot_count = 2 * ((holding + devices - 1) // devices)
    views, _, taps = psf.shape
    planes = estimate.shape[0]
    target = tile_dest[:, 0]
    earlier = (target[None, :] == target[:, None]) & (
        jnp.arange(holding)[None, :] < jnp.arange(holding)[:, None]
    )
    rank = jnp.sum(earlier.astype(jnp.int32), axis=1)
    where_to = target * slot_count + rank
    placing = where_to[None, :] == jnp.arange(devices * slot_count)[:, None]
    pick = jnp.sum(jnp.where(placing, jnp.arange(holding, dtype=jnp.int32)[None, :], 0), axis=1)
    labels = jnp.sum(jnp.where(placing, tile_slot[None, :] + 1, 0), axis=1) - 1
    packed = pack(pick, tiles)
    exchange = functools.partial(
        lax.all_to_all, axis_name=("gy", "gx"), split_axis=0, concat_axis=0, tiled=True
    )
    got_labels = exchange(labels.reshape(devices, slot_count)).reshape(-1)
    grid = (lax.axis_size("gy"), lax.axis_size("gx"))
    volume = jax.ShapeDtypeStruct(estimate.shape, jnp.float32)
    framed = jax.ShapeDtypeStruct((planes, side + 2 * PAD, 2 * side), jnp.bfloat16)
    rim, folds = rim_scratch(planes, side), fold_scratch(planes, side)
    (wide,) = rim_call(functools.partial(first_kernel, grid), "rim_first", 0, [framed], folds + rim, [estimate])
    packed, wide, got_labels = lax.optimization_barrier((packed, wide, got_labels))
    got_tiles = exchange(packed.reshape(devices, slot_count, side, side)).reshape(-1, side, side)

    kernel = (psf / jnp.sum(psf, axis=2, keepdims=True)).astype(jnp.bfloat16).astype(jnp.float32)
    bx, by, kz, kf, fy, fx = bands(kernel.reshape(views * 3, taps), planes, side)

    sorting = got_labels[None, :] == jnp.arange(views * planes)[:, None]
    counted = jnp.sum(sorting.astype(jnp.float32), axis=1).reshape(views, planes)
    count = jnp.broadcast_to(counted[:, :, None], (views, planes, side))
    seen = None
    for repeat_index in range(ITERS):
        along = sides(wide, bx, by)
        if seen is None:
            seen = observe(got_labels, got_tiles, views * planes).reshape(views, planes, side, side)
        back = depth(along, seen, count, kz, kf)
        parts = spread(back, fy, fx)
        if repeat_index + 1 < ITERS:
            estimate, wide = rim_call(
                functools.partial(between_kernel, grid, views), "rim_between", 1,
                [volume, framed], rim + folds + rim, [estimate, *parts],
            )
        else:
            (total,) = rim_call(functools.partial(last_kernel, grid), "rim_last", 2, [volume], rim, parts)
            estimate = estimate * total / views
    return estimate


def solution(mesh):
    placed = (
        P(("gy", "gx"), None, None),
        P(("gy", "gx"), None),
        P(("gy", "gx")),
        P(),
        P(None, "gy", "gx"),
    )
    return jax.shard_map(
        local, mesh=mesh, in_specs=placed, out_specs=P(None, "gy", "gx"), check_vma=False
    )
```

```python
import functools

import jax
import jax.numpy as jnp
from jax import lax
from jax.experimental import pallas as pl
from jax.experimental.pallas import tpu as pltpu
from jax.sharding import PartitionSpec as P

ITERS = 2
PAD = 16
VMEM = 56 * 1024 * 1024

damping = 0.05


def coordinate(index, side):
    return jnp.where(index < side, index, jnp.where(index < side + PAD, index - side - PAD, index - PAD))


def toeplitz(taps_ref, row, offset):
    def add(t, held):
        return jnp.where(offset == t, taps_ref[row, t], held)

    return lax.fori_loop(0, taps_ref.shape[1], add, jnp.zeros(offset.shape, jnp.float32))


def bands_kernel(reach, planes, side, taps_ref, bx_ref, by_ref, kz_ref, kf_ref, fy_ref, fx_ref):
    views = by_ref.shape[0]
    ext = side + 2 * PAD
    wide = fx_ref.shape[1]
    iota = lambda shape, dim: lax.broadcasted_iota(jnp.int32, shape, dim)
    tall_off = coordinate(iota((ext, side), 0), side) - iota((ext, side), 1) + reach
    long_ext = iota((side, wide), 1)
    long_off = coordinate(long_ext, side) - iota((side, wide), 0) + reach
    long_off = jnp.where(long_ext < ext, long_off, -1)
    lanes = 128
    z_col = iota((planes, lanes), 1)
    z_diff = z_col - iota((planes, lanes), 0)
    full = planes * 8
    spread_l = (iota((full, planes), 0) // 8 == iota((full, planes), 1)).astype(jnp.bfloat16)
    spread_r = (iota((lanes, full), 1) // 8 == iota((lanes, full), 0)).astype(jnp.bfloat16)
    same = iota((full, full), 0) % 8 == iota((full, full), 1) % 8

    def kron(row, offset):
        small = toeplitz(taps_ref, row, offset).astype(jnp.bfloat16)
        right = jnp.dot(small, spread_r, preferred_element_type=jnp.float32).astype(jnp.bfloat16)
        both = jnp.dot(spread_l, right, preferred_element_type=jnp.float32)
        return jnp.where(same, both, 0.0).astype(jnp.bfloat16)

    for v in range(views):
        kz_ref[v] = kron(3 * v, jnp.where(z_col < planes, z_diff + reach, -1))
        kf_ref[v] = kron(3 * v, jnp.where(z_col < planes, reach - z_diff, -1))
        tall_y = toeplitz(taps_ref, 3 * v + 1, tall_off)
        long_y = toeplitz(taps_ref, 3 * v + 1, long_off)
        fy_ref[v] = tall_y.astype(jnp.bfloat16)
        by_ref[v] = long_y[:, :ext].astype(jnp.bfloat16)
        tall_x = toeplitz(taps_ref, 3 * v + 2, tall_off)
        long_x = toeplitz(taps_ref, 3 * v + 2, long_off)
        bx_ref[:ext, v * side : (v + 1) * side] = tall_x.astype(jnp.bfloat16)
        bx_ref[ext:, v * side : (v + 1) * side] = jnp.zeros((wide - ext, side), jnp.bfloat16)
        fx_ref[v * side : (v + 1) * side, :] = long_x.astype(jnp.bfloat16)


def bands(taps, planes, side):
    views = taps.shape[0] // 3
    ext = side + 2 * PAD
    shapes = [
        (2 * side, views * side),
        (views, side, ext),
        (views, planes * 8, planes * 8),
        (views, planes * 8, planes * 8),
        (views, ext, side),
        (views * side, 2 * side),
    ]
    return pl.pallas_call(
        functools.partial(bands_kernel, (taps.shape[1] - 1) // 2, planes, side),
        out_shape=[jax.ShapeDtypeStruct(s, jnp.bfloat16) for s in shapes],
        in_specs=[pl.BlockSpec(memory_space=pltpu.SMEM)],
        out_specs=[pl.BlockSpec(memory_space=pltpu.VMEM)] * len(shapes),
        compiler_params=pltpu.CompilerParams(vmem_limit_bytes=VMEM),
        name="bands",
    )(taps)


def pack_kernel(pick_ref, tiles_ref, out_ref, sem):
    count = out_ref.shape[0]

    def send(slot, carry):
        pltpu.make_async_copy(tiles_ref.at[pick_ref[slot]], out_ref.at[slot], sem).start()
        return carry

    lax.fori_loop(0, count, send, 0)
    pltpu.make_async_copy(out_ref, out_ref, sem).wait()


def pack(pick, tiles):
    count = pick.shape[0]
    return pl.pallas_call(
        pack_kernel,
        out_shape=jax.ShapeDtypeStruct((count,) + tiles.shape[1:], tiles.dtype),
        in_specs=[pl.BlockSpec(memory_space=pltpu.SMEM), pl.BlockSpec(memory_space=pltpu.VMEM)],
        out_specs=pl.BlockSpec(memory_space=pl.ANY),
        scratch_shapes=[pltpu.SemaphoreType.DMA],
        compiler_params=pltpu.CompilerParams(vmem_limit_bytes=VMEM),
        name="pack",
    )(pick, tiles)


def sides_kernel(wide_ref, bx_ref, by_ref, out_ref):
    views, planes, side, _ = out_ref.shape
    for z in range(planes):
        along_x = jnp.dot(wide_ref[z], bx_ref[...], preferred_element_type=jnp.float32).astype(jnp.bfloat16)
        for v in range(views):
            out_ref[v, z] = jnp.dot(
                by_ref[v], along_x[:, v * side : (v + 1) * side], preferred_element_type=jnp.float32
            ).astype(jnp.bfloat16)


def sides(wide, bx, by):
    planes, ext, _ = wide.shape
    views, side, _ = by.shape
    chunk = 4
    macs = planes * ext * ext * side * views + planes * views * side * side * ext
    return pl.pallas_call(
        sides_kernel,
        out_shape=jax.ShapeDtypeStruct((views, planes, side, side), jnp.bfloat16),
        grid=(planes // chunk,),
        in_specs=[
            pl.BlockSpec((chunk,) + wide.shape[1:], lambda i: (i, 0, 0)),
            pl.BlockSpec(bx.shape, lambda i: (0, 0)),
            pl.BlockSpec(by.shape, lambda i: (0, 0, 0)),
        ],
        out_specs=pl.BlockSpec((views, chunk, side, side), lambda i: (0, i, 0, 0)),
        compiler_params=pltpu.CompilerParams(vmem_limit_bytes=VMEM),
        cost_estimate=pl.CostEstimate(flops=2 * macs, bytes_accessed=views * planes * side * side * 3, transcendentals=0),
        name="sides",
    )(wide, bx, by)


def depth(along, seen, count_ref, kz, kf, back_ref, v):
    planes, side, _ = along.shape
    full = planes * 8
    count = jnp.broadcast_to(count_ref[0][:, None, :], (planes, 8, side)).reshape(full, side)
    count = jnp.concatenate([count, count], axis=1)

    def both(values):
        return jnp.concatenate([values[:, :8].reshape(full, side), values[:, 8:].reshape(full, side)], axis=1)

    for p in range(side // 16):
        spot = slice(p * 16, p * 16 + 16)
        stack = both(along[:, spot].astype(jnp.float32)).astype(jnp.bfloat16)
        blur = jnp.dot(kz, stack, preferred_element_type=jnp.float32)
        ratio = ((both(seen(spot)) + damping) / (count * blur + damping)).astype(jnp.bfloat16)
        back = jnp.dot(kf, ratio, preferred_element_type=jnp.float32)
        back_ref[v, :, spot] = jnp.concatenate(
            [back[:, :side].reshape(planes, 8, side), back[:, side:].reshape(planes, 8, side)], axis=1
        ).astype(jnp.bfloat16)


def fold_lanes(values, start):
    lane = lax.broadcasted_iota(jnp.int32, values[0].shape, 1)
    held = jnp.zeros(values[0].shape, jnp.float32)
    for k, one in enumerate(values):
        held = jnp.where(lane // PAD == k, pltpu.roll(one, (PAD * k - start) % 128, 1), held)
    return held


def unfold_lanes(held, k, start):
    lane = lax.broadcasted_iota(jnp.int32, held.shape, 1)
    return jnp.where(lane // PAD == start // PAD, pltpu.roll(held, (start - PAD * k) % 128, 1), 0.0)


def spread(fold, back_ref, fy_ref, fx_ref, in_ref, ys_ref, xl_ref, xr_ref):
    views, _, side, _ = back_ref.shape
    rims = []
    for z in range(8):
        wide = jnp.concatenate(
            [
                jnp.dot(fy_ref[v], back_ref[v, fold * 8 + z], preferred_element_type=jnp.float32).astype(jnp.bfloat16)
                for v in range(views)
            ],
            axis=1,
        )
        part = jnp.dot(wide, fx_ref[...], preferred_element_type=jnp.float32)
        in_ref[z] = part[:side, :side]
        ys_ref[z] = part[side:, :side].astype(jnp.bfloat16)
        rims.append(part[:, side:])
    xl_ref[0] = fold_lanes(rims, 0).astype(jnp.bfloat16)
    xr_ref[0] = fold_lanes(rims, PAD).astype(jnp.bfloat16)


def turn_kernel(chunk, loads, label_ref, tiles_ref, along_ref, count_ref, kz_ref, kf_ref, fy_ref, fx_ref, *outs):
    *parts, seen_ref, back_ref, held_ref = outs
    step = pl.program_id(0)
    views, planes = back_ref.shape[:2]

    if loads:
        @pl.when(step == 0)
        def _():
            def clear(plane, carry):
                held_ref[plane] = jnp.zeros(held_ref.shape[1:], jnp.float32)
                return carry

            lax.fori_loop(0, views * planes, clear, 0)

        @pl.when(step < loads)
        def _():
            def add(i, carry):
                label = label_ref[step * chunk + i]

                @pl.when(label >= 0)
                def _():
                    held_ref[label] += tiles_ref[i].astype(jnp.float32)

                return carry

            lax.fori_loop(0, chunk, add, 0)

    @pl.when((step >= loads) & (step < loads + views))
    def _():
        v = step - loads
        if loads:
            base = pl.multiple_of(v * planes, planes)
            seen_ref[0] = held_ref[pl.ds(base, planes)].astype(jnp.bfloat16)
            seen = lambda spot: held_ref[pl.ds(base, planes), spot]
        else:
            seen = lambda spot: seen_ref[0, :, spot].astype(jnp.float32)
        depth(along_ref.at[0], seen, count_ref, kz_ref[0], kf_ref[0], back_ref, v)

    @pl.when(step >= loads + views)
    def _():
        spread(step - loads - views, back_ref, fy_ref, fx_ref, *parts)


def later_kernel(along_ref, seen_ref, count_ref, kz_ref, kf_ref, fy_ref, fx_ref, *outs):
    *parts, back_ref = outs
    turn_kernel(0, 0, None, None, along_ref, count_ref, kz_ref, kf_ref, fy_ref, fx_ref, *parts, seen_ref, back_ref, None)


def turn(along, count, kz, kf, fy, fx, seen=None, labels=None, tiles=None):
    views, planes, side, _ = along.shape
    ext = fy.shape[1]
    folds = planes // 8
    chunk = 32
    loads = 0 if tiles is None else tiles.shape[0] // chunk
    view = lambda i: jnp.clip(i - loads, 0, views - 1)
    fold = lambda i: jnp.maximum(i - loads - views, 0)
    per_view = lambda shape: pl.BlockSpec((1,) + shape[1:], lambda i: (view(i),) + (0,) * (len(shape) - 1))
    per_fold = lambda shape: pl.BlockSpec(shape, lambda i: (fold(i), 0, 0))
    whole = lambda shape: pl.BlockSpec(shape, lambda i: (0,) * len(shape))
    volume = per_view(along.shape)
    shapes = [
        jax.ShapeDtypeStruct((planes, side, side), jnp.float32),
        jax.ShapeDtypeStruct((planes, 2 * PAD, side), jnp.bfloat16),
        jax.ShapeDtypeStruct((folds, ext, side), jnp.bfloat16),
        jax.ShapeDtypeStruct((folds, ext, side), jnp.bfloat16),
    ]
    out_specs = [per_fold((8, side, side)), per_fold((8, 2 * PAD, side)), per_fold((1, ext, side)), per_fold((1, ext, side))]
    filters = [per_view(count.shape), per_view(kz.shape), per_view(kf.shape), whole(fy.shape), whole(fx.shape)]
    scratch = [pltpu.VMEM((views, planes, side, side), jnp.bfloat16)]
    if loads:
        shapes.append(jax.ShapeDtypeStruct(along.shape, jnp.bfloat16))
        out_specs.append(volume)
        in_specs = [
            pl.BlockSpec(memory_space=pltpu.SMEM),
            pl.BlockSpec((chunk, side, side), lambda i: (jnp.minimum(i, loads - 1), 0, 0)),
            volume,
        ]
        args = [labels, tiles, along]
        scratch.append(pltpu.VMEM((views * planes, side, side), jnp.float32))
        kernel = functools.partial(turn_kernel, chunk, loads)
    else:
        in_specs = [volume, volume]
        args = [along, seen]
        kernel = later_kernel
    return pl.pallas_call(
        kernel,
        out_shape=shapes,
        grid=(loads + views + folds,),
        in_specs=in_specs + filters,
        out_specs=out_specs,
        scratch_shapes=scratch,
        compiler_params=pltpu.CompilerParams(vmem_limit_bytes=VMEM),
        name="turn",
    )(*args, count, kz, kf, fy, fx)


NEAR = [(-1, 0), (1, 0), (0, -1), (0, 1), (-1, -1), (1, -1), (-1, 1), (1, 1)]


def inside(grid, dy, dx):
    ny, nx = grid
    y = lax.axis_index("gy") + dy
    x = lax.axis_index("gx") + dx
    return (y >= 0) & (y < ny) & (x >= 0) & (x < nx), (y, x)


def greet(grid):
    barrier = pltpu.get_barrier_semaphore()
    for dy, dx in NEAR:
        there, where = inside(grid, dy, dx)

        @pl.when(there)
        def _():
            pl.semaphore_signal(barrier, inc=1, device_id=where, device_id_type=pl.DeviceIdType.MESH)

    ny, nx = grid
    y, x = lax.axis_index("gy"), lax.axis_index("gx")
    tall = 3 - (y == 0).astype(jnp.int32) - (y == ny - 1).astype(jnp.int32)
    broad = 3 - (x == 0).astype(jnp.int32) - (x == nx - 1).astype(jnp.int32)
    pl.semaphore_wait(barrier, tall * broad - 1)


def swap(grid, moves, send_sems, recv_sems):
    def copy(i, where):
        source, dest = moves[i]
        return pltpu.make_async_remote_copy(
            src_ref=source, dst_ref=dest, send_sem=send_sems.at[i], recv_sem=recv_sems.at[i],
            device_id=where, device_id_type=pl.DeviceIdType.MESH,
        )

    for i, (dy, dx) in enumerate(NEAR):
        there, where = inside(grid, dy, dx)

        @pl.when(there)
        def _():
            copy(i, where).start()

    for i, (dy, dx) in enumerate(NEAR):
        there, where = inside(grid, -dy, -dx)

        @pl.when(there)
        def _():
            copy(i, where).wait_recv()

        @pl.when(jnp.logical_not(there))
        def _():
            dest = moves[i][1]
            dest[...] = jnp.zeros(dest.shape, dest.dtype)

    for i, (dy, dx) in enumerate(NEAR):
        there, where = inside(grid, dy, dx)

        @pl.when(there)
        def _():
            copy(i, where).wait_send()


def widen(grid, fresh, wide_ref, left, right, rows, from_left, from_right, send_sems, recv_sems):
    planes, ext, _ = wide_ref.shape
    side = ext - 2 * PAD

    def cut(p, carry):
        values = []
        for k in range(8):
            plane = fresh(p * 8 + k)
            values.append(plane)
            wide_ref[p * 8 + k, :side, :side] = plane.astype(jnp.bfloat16)
        left[p] = fold_lanes(values, 0).astype(jnp.bfloat16)
        right[p] = fold_lanes(values, side - PAD).astype(jnp.bfloat16)
        return carry

    lax.fori_loop(0, planes // 8, cut, 0)
    first, last = pl.ds(0, PAD), pl.ds(side - PAD, PAD)
    whole, before, after = pl.ds(0, side), pl.ds(side, PAD), pl.ds(side + PAD, PAD)
    lanes = pl.ds(0, side)
    moves = [
        (wide_ref.at[:, first, lanes], rows.at[:, pl.ds(PAD, PAD)]),
        (wide_ref.at[:, last, lanes], rows.at[:, pl.ds(0, PAD)]),
        (left, from_right.at[:, whole]),
        (right, from_left.at[:, whole]),
        (left.at[:, first], from_right.at[:, after]),
        (left.at[:, last], from_right.at[:, before]),
        (right.at[:, first], from_left.at[:, after]),
        (right.at[:, last], from_left.at[:, before]),
    ]
    swap(grid, moves, send_sems, recv_sems)

    def paste(p, carry):
        low = from_left[p].astype(jnp.float32)
        high = from_right[p].astype(jnp.float32)
        for k in range(8):
            rim = unfold_lanes(low, k, 0) + unfold_lanes(high, k, PAD)
            wide_ref[p * 8 + k, :, side:] = rim.astype(jnp.bfloat16)
            wide_ref[p * 8 + k, side:, :side] = rows[p * 8 + k]
        return carry

    lax.fori_loop(0, planes // 8, paste, 0)


def rim_scratch(planes, side):
    ext = side + 2 * PAD
    return [
        pltpu.VMEM((planes, 2 * PAD, side), jnp.bfloat16),
        pltpu.VMEM((planes // 8, ext, side), jnp.bfloat16),
        pltpu.VMEM((planes // 8, ext, side), jnp.bfloat16),
        pltpu.SemaphoreType.DMA((8,)),
        pltpu.SemaphoreType.DMA((8,)),
    ]


def fold_scratch(planes, side):
    return [pltpu.VMEM((planes // 8, side, side), jnp.bfloat16)] * 2


def gather(grid, in_ref, ys_ref, xl_ref, xr_ref, rows, from_left, from_right, send_sems, recv_sems):
    planes, side, _ = in_ref.shape
    whole, before, after = pl.ds(0, side), pl.ds(side, PAD), pl.ds(side + PAD, PAD)
    first, second = pl.ds(0, PAD), pl.ds(PAD, PAD)
    moves = [
        (ys_ref.at[:, first], rows.at[:, second]),
        (ys_ref.at[:, second], rows.at[:, first]),
        (xl_ref.at[:, whole], from_right.at[:, whole]),
        (xr_ref.at[:, whole], from_left.at[:, whole]),
        (xl_ref.at[:, before], from_right.at[:, after]),
        (xl_ref.at[:, after], from_right.at[:, before]),
        (xr_ref.at[:, before], from_left.at[:, after]),
        (xr_ref.at[:, after], from_left.at[:, before]),
    ]
    swap(grid, moves, send_sems, recv_sems)


def totals(z, p, k, in_ref, rows, from_left, from_right):
    side = in_ref.shape[1]
    gap = jnp.zeros((side - 2 * PAD, side), jnp.float32)
    edge = rows[z].astype(jnp.float32)

    def rim(held, start):
        held = held.astype(jnp.float32)
        body = held[:side] + jnp.concatenate([held[side : side + PAD], gap, held[side + PAD :]], axis=0)
        return unfold_lanes(body, k, start)

    total = in_ref[z] + jnp.concatenate([edge[:PAD], gap, edge[PAD:]], axis=0)
    return total + rim(from_left[p], 0) + rim(from_right[p], side - PAD)


def first_kernel(grid, est_ref, wide_ref, left, right, *rim):
    greet(grid)
    widen(grid, lambda z: est_ref[z], wide_ref, left, right, *rim)


def between_kernel(grid, views, est_ref, in_ref, ys_ref, xl_ref, xr_ref, new_ref, wide_ref, *scratch):
    greet(grid)
    rim, (left, right), again = scratch[:5], scratch[5:7], scratch[7:]
    gather(grid, in_ref, ys_ref, xl_ref, xr_ref, *rim)

    def update(p, carry):
        for k in range(8):
            z = p * 8 + k
            new_ref[z] = est_ref[z] * totals(z, p, k, in_ref, *rim[:3]) / views
        return carry

    lax.fori_loop(0, est_ref.shape[0] // 8, update, 0)
    widen(grid, lambda z: new_ref[z], wide_ref, left, right, *again)


def last_kernel(grid, in_ref, ys_ref, xl_ref, xr_ref, out_ref, *rim):
    greet(grid)
    gather(grid, in_ref, ys_ref, xl_ref, xr_ref, *rim)

    def update(p, carry):
        for k in range(8):
            z = p * 8 + k
            out_ref[z] = totals(z, p, k, in_ref, *rim[:3])
        return carry

    lax.fori_loop(0, in_ref.shape[0] // 8, update, 0)


def rim_call(kernel, name, number, shapes, scratch, args):
    held = pl.BlockSpec(memory_space=pltpu.VMEM)
    return pl.pallas_call(
        kernel,
        out_shape=shapes,
        in_specs=[held] * len(args),
        out_specs=[held] * len(shapes),
        scratch_shapes=scratch,
        compiler_params=pltpu.CompilerParams(
            vmem_limit_bytes=VMEM, collective_id=number, has_side_effects=True
        ),
        name=name,
    )(*args)


def local(tiles, tile_dest, tile_slot, psf, estimate):
    devices = lax.axis_size("gy") * lax.axis_size("gx")
    holding, side, _ = tiles.shape
    slot_count = 2 * ((holding + devices - 1) // devices)
    views, _, taps = psf.shape
    planes = estimate.shape[0]
    target = tile_dest[:, 0]
    earlier = (target[None, :] == target[:, None]) & (
        jnp.arange(holding)[None, :] < jnp.arange(holding)[:, None]
    )
    rank = jnp.sum(earlier.astype(jnp.int32), axis=1)
    where_to = target * slot_count + rank
    placing = where_to[None, :] == jnp.arange(devices * slot_count)[:, None]
    pick = jnp.sum(jnp.where(placing, jnp.arange(holding, dtype=jnp.int32)[None, :], 0), axis=1)
    labels = jnp.sum(jnp.where(placing, tile_slot[None, :] + 1, 0), axis=1) - 1
    packed = pack(pick, tiles)
    exchange = functools.partial(
        lax.all_to_all, axis_name=("gy", "gx"), split_axis=0, concat_axis=0, tiled=True
    )
    me = lax.axis_index("gy") * lax.axis_size("gx") + lax.axis_index("gx")
    everyones = lax.all_gather(labels.reshape(devices, slot_count), ("gy", "gx"))
    got_labels = lax.dynamic_index_in_dim(everyones, me, axis=1, keepdims=False).reshape(-1)
    grid = (lax.axis_size("gy"), lax.axis_size("gx"))
    volume = jax.ShapeDtypeStruct(estimate.shape, jnp.float32)
    framed = jax.ShapeDtypeStruct((planes, side + 2 * PAD, 2 * side), jnp.bfloat16)
    rim, folds = rim_scratch(planes, side), fold_scratch(planes, side)
    (wide,) = rim_call(functools.partial(first_kernel, grid), "rim_first", 0, [framed], folds + rim, [estimate])
    packed, wide = lax.optimization_barrier((packed, wide))
    got_tiles = exchange(packed.reshape(devices, slot_count, side, side)).reshape(-1, side, side)

    kernel = (psf / jnp.sum(psf, axis=2, keepdims=True)).astype(jnp.bfloat16).astype(jnp.float32)
    bx, by, kz, kf, fy, fx = bands(kernel.reshape(views * 3, taps), planes, side)

    sorting = got_labels[None, :] == jnp.arange(views * planes)[:, None]
    counted = jnp.sum(sorting.astype(jnp.float32), axis=1).reshape(views, planes)
    count = jnp.broadcast_to(counted[:, :, None], (views, planes, side))
    seen = None
    for repeat_index in range(ITERS):
        along = sides(wide, bx, by)
        if seen is None:
            *parts, seen = turn(along, count, kz, kf, fy, fx, labels=got_labels, tiles=got_tiles)
        else:
            parts = turn(along, count, kz, kf, fy, fx, seen=seen)
        if repeat_index + 1 < ITERS:
            estimate, wide = rim_call(
                functools.partial(between_kernel, grid, views), "rim_between", 1,
                [volume, framed], rim + folds + rim, [estimate, *parts],
            )
        else:
            (total,) = rim_call(functools.partial(last_kernel, grid), "rim_last", 2, [volume], rim, parts)
            estimate = estimate * total / views
    return estimate


def solution(mesh):
    placed = (
        P(("gy", "gx"), None, None),
        P(("gy", "gx"), None),
        P(("gy", "gx")),
        P(),
        P(None, "gy", "gx"),
    )
    return jax.shard_map(
        local, mesh=mesh, in_specs=placed, out_specs=P(None, "gy", "gx"), check_vma=False
    )
```

```python
import functools

import jax
import jax.numpy as jnp
from jax import lax
from jax.experimental import pallas as pl
from jax.experimental.pallas import tpu as pltpu
from jax.sharding import PartitionSpec as P

ITERS = 2
PAD = 16
VMEM = 56 * 1024 * 1024

damping = 0.05


def coordinate(index, side):
    return jnp.where(index < side, index, jnp.where(index < side + PAD, index - side - PAD, index - PAD))


def toeplitz(taps_ref, row, offset):
    def add(t, held):
        return jnp.where(offset == t, taps_ref[row, t], held)

    return lax.fori_loop(0, taps_ref.shape[1], add, jnp.zeros(offset.shape, jnp.float32))


def bands_kernel(reach, planes, side, taps_ref, bx_ref, by_ref, kz_ref, kf_ref, fy_ref, fx_ref):
    views = by_ref.shape[0]
    ext = side + 2 * PAD
    wide = fx_ref.shape[1]
    iota = lambda shape, dim: lax.broadcasted_iota(jnp.int32, shape, dim)
    tall_off = coordinate(iota((ext, side), 0), side) - iota((ext, side), 1) + reach
    long_ext = iota((side, wide), 1)
    long_off = coordinate(long_ext, side) - iota((side, wide), 0) + reach
    long_off = jnp.where(long_ext < ext, long_off, -1)
    lanes = 128
    z_col = iota((planes, lanes), 1)
    z_diff = z_col - iota((planes, lanes), 0)
    full = planes * 8
    spread_l = (iota((full, planes), 0) // 8 == iota((full, planes), 1)).astype(jnp.bfloat16)
    spread_r = (iota((lanes, full), 1) // 8 == iota((lanes, full), 0)).astype(jnp.bfloat16)
    same = iota((full, full), 0) % 8 == iota((full, full), 1) % 8

    def kron(row, offset):
        small = toeplitz(taps_ref, row, offset).astype(jnp.bfloat16)
        right = jnp.dot(small, spread_r, preferred_element_type=jnp.float32).astype(jnp.bfloat16)
        both = jnp.dot(spread_l, right, preferred_element_type=jnp.float32)
        return jnp.where(same, both, 0.0).astype(jnp.bfloat16)

    for v in range(views):
        kz_ref[v] = kron(3 * v, jnp.where(z_col < planes, z_diff + reach, -1))
        kf_ref[v] = kron(3 * v, jnp.where(z_col < planes, reach - z_diff, -1))
        tall_y = toeplitz(taps_ref, 3 * v + 1, tall_off)
        long_y = toeplitz(taps_ref, 3 * v + 1, long_off)
        fy_ref[v] = tall_y.astype(jnp.bfloat16)
        by_ref[v] = long_y[:, :ext].astype(jnp.bfloat16)
        tall_x = toeplitz(taps_ref, 3 * v + 2, tall_off)
        long_x = toeplitz(taps_ref, 3 * v + 2, long_off)
        bx_ref[:ext, v * side : (v + 1) * side] = tall_x.astype(jnp.bfloat16)
        bx_ref[ext:, v * side : (v + 1) * side] = jnp.zeros((wide - ext, side), jnp.bfloat16)
        fx_ref[v * side : (v + 1) * side, :] = long_x.astype(jnp.bfloat16)


def bands(taps, planes, side):
    views = taps.shape[0] // 3
    ext = side + 2 * PAD
    shapes = [
        (2 * side, views * side),
        (views, side, ext),
        (views, planes * 8, planes * 8),
        (views, planes * 8, planes * 8),
        (views, ext, side),
        (views * side, 2 * side),
    ]
    return pl.pallas_call(
        functools.partial(bands_kernel, (taps.shape[1] - 1) // 2, planes, side),
        out_shape=[jax.ShapeDtypeStruct(s, jnp.bfloat16) for s in shapes],
        in_specs=[pl.BlockSpec(memory_space=pltpu.SMEM)],
        out_specs=[pl.BlockSpec(memory_space=pltpu.VMEM)] * len(shapes),
        compiler_params=pltpu.CompilerParams(vmem_limit_bytes=VMEM),
        name="bands",
    )(taps)


def pack_kernel(pick_ref, tiles_ref, out_ref, sem):
    count = out_ref.shape[0]

    def send(slot, carry):
        pltpu.make_async_copy(tiles_ref.at[pick_ref[slot]], out_ref.at[slot], sem).start()
        return carry

    lax.fori_loop(0, count, send, 0)
    pltpu.make_async_copy(out_ref, out_ref, sem).wait()


def pack(pick, tiles):
    count = pick.shape[0]
    return pl.pallas_call(
        pack_kernel,
        out_shape=jax.ShapeDtypeStruct((count,) + tiles.shape[1:], tiles.dtype),
        in_specs=[pl.BlockSpec(memory_space=pltpu.SMEM), pl.BlockSpec(memory_space=pltpu.VMEM)],
        out_specs=pl.BlockSpec(memory_space=pl.ANY),
        scratch_shapes=[pltpu.SemaphoreType.DMA],
        compiler_params=pltpu.CompilerParams(vmem_limit_bytes=VMEM),
        name="pack",
    )(pick, tiles)


def sides_kernel(wide_ref, bx_ref, by_ref, out_ref):
    views, planes, side, _ = out_ref.shape
    along_y = [
        jnp.dot(by_ref[...], wide_ref[z], preferred_element_type=jnp.float32).astype(jnp.bfloat16)
        for z in range(planes)
    ]
    for v in range(views):
        spot = slice(v * side, (v + 1) * side)
        stack = jnp.concatenate([one[spot] for one in along_y], axis=0)
        both = jnp.dot(stack, bx_ref[:, spot], preferred_element_type=jnp.float32)
        out_ref[v] = both.astype(jnp.bfloat16).reshape(planes, side, side)


def sides(wide, bx, by):
    planes, ext, _ = wide.shape
    views, side, _ = by.shape
    by = by.reshape(views * side, ext)
    chunk = 4
    macs = planes * ext * ext * side * views + planes * views * side * side * ext
    return pl.pallas_call(
        sides_kernel,
        out_shape=jax.ShapeDtypeStruct((views, planes, side, side), jnp.bfloat16),
        grid=(planes // chunk,),
        in_specs=[
            pl.BlockSpec((chunk,) + wide.shape[1:], lambda i: (i, 0, 0)),
            pl.BlockSpec(bx.shape, lambda i: (0, 0)),
            pl.BlockSpec(by.shape, lambda i: (0, 0)),
        ],
        out_specs=pl.BlockSpec((views, chunk, side, side), lambda i: (0, i, 0, 0)),
        compiler_params=pltpu.CompilerParams(vmem_limit_bytes=VMEM),
        cost_estimate=pl.CostEstimate(flops=2 * macs, bytes_accessed=views * planes * side * side * 3, transcendentals=0),
        name="sides",
    )(wide, bx, by)


def halves(values):
    planes, _, side = values.shape
    full = planes * 8
    return jnp.concatenate([values[:, :8].reshape(full, side), values[:, 8:].reshape(full, side)], axis=1)


def below(along, count_ref, kz, spot):
    planes, side, _ = along.shape
    full = planes * 8
    count = jnp.broadcast_to(count_ref[0][:, None, :], (planes, 8, side)).reshape(full, side)
    stack = halves(along[:, spot].astype(jnp.float32)).astype(jnp.bfloat16)
    blur = jnp.dot(kz, stack, preferred_element_type=jnp.float32)
    return jnp.concatenate([count, count], axis=1) * blur + damping


def weigh_kernel(along_ref, count_ref, kz_ref, out_ref):
    for p in range(out_ref.shape[1]):
        out_ref[0, p] = 1.0 / below(along_ref.at[0], count_ref, kz_ref[0], slice(p * 16, p * 16 + 16))


def weigh(along, count, kz):
    views, planes, side, _ = along.shape
    pairs, full = side // 16, planes * 8
    per_view = lambda shape: pl.BlockSpec((1,) + shape[1:], lambda i: (i,) + (0,) * (len(shape) - 1))
    shape = (views, pairs, full, 2 * side)
    return pl.pallas_call(
        weigh_kernel,
        out_shape=jax.ShapeDtypeStruct(shape, jnp.float32),
        grid=(views,),
        in_specs=[per_view(along.shape), per_view(count.shape), per_view(kz.shape)],
        out_specs=per_view(shape),
        compiler_params=pltpu.CompilerParams(vmem_limit_bytes=VMEM),
        name="weigh",
    )(along, count, kz)


def depth(ratio, kf, back_ref, v):
    _, planes, side, _ = back_ref.shape
    for p in range(side // 16):
        spot = slice(p * 16, p * 16 + 16)
        back = jnp.dot(kf, ratio(p, spot).astype(jnp.bfloat16), preferred_element_type=jnp.float32)
        back_ref[v, :, spot] = jnp.concatenate(
            [back[:, :side].reshape(planes, 8, side), back[:, side:].reshape(planes, 8, side)], axis=1
        ).astype(jnp.bfloat16)


def fold_lanes(values, start):
    lane = lax.broadcasted_iota(jnp.int32, values[0].shape, 1)
    held = jnp.zeros(values[0].shape, jnp.float32)
    for k, one in enumerate(values):
        held = jnp.where(lane // PAD == k, pltpu.roll(one, (PAD * k - start) % 128, 1), held)
    return held


def unfold_lanes(held, k, start):
    lane = lax.broadcasted_iota(jnp.int32, held.shape, 1)
    return jnp.where(lane // PAD == start // PAD, pltpu.roll(held, (start - PAD * k) % 128, 1), 0.0)


def spread(fold, back_ref, fy_ref, fx_ref, in_ref, ys_ref, xl_ref, xr_ref):
    views, _, side, _ = back_ref.shape
    rims = []
    for z in range(8):
        wide = jnp.concatenate(
            [
                jnp.dot(fy_ref[v], back_ref[v, fold * 8 + z], preferred_element_type=jnp.float32).astype(jnp.bfloat16)
                for v in range(views)
            ],
            axis=1,
        )
        part = jnp.dot(wide, fx_ref[...], preferred_element_type=jnp.float32)
        in_ref[z] = part[:side, :side]
        ys_ref[z] = part[side:, :side].astype(jnp.bfloat16)
        rims.append(part[:, side:])
    xl_ref[0] = fold_lanes(rims, 0).astype(jnp.bfloat16)
    xr_ref[0] = fold_lanes(rims, PAD).astype(jnp.bfloat16)


def first_turn(chunk, loads, label_ref, tiles_ref, weight_ref, kf_ref, fy_ref, fx_ref, *outs):
    *parts, seen_ref, back_ref, held_ref = outs
    step = pl.program_id(0)
    views, planes = back_ref.shape[:2]

    @pl.when(step == 0)
    def _():
        def clear(plane, carry):
            held_ref[plane] = jnp.zeros(held_ref.shape[1:], jnp.float32)
            return carry

        lax.fori_loop(0, views * planes, clear, 0)

    @pl.when(step < loads)
    def _():
        def add(i, carry):
            label = label_ref[step * chunk + i]

            @pl.when(label >= 0)
            def _():
                held_ref[label] += tiles_ref[i].astype(jnp.float32)

            return carry

        lax.fori_loop(0, chunk, add, 0)

    @pl.when((step >= loads) & (step < loads + views))
    def _():
        v = step - loads
        base = pl.multiple_of(v * planes, planes)

        def ratio(p, spot):
            seen = held_ref[pl.ds(base, planes), spot]
            seen_ref[0, :, spot] = seen.astype(jnp.bfloat16)
            return (halves(seen) + damping) * weight_ref[0, p]

        depth(ratio, kf_ref[0], back_ref, v)

    @pl.when(step >= loads + views)
    def _():
        spread(step - loads - views, back_ref, fy_ref, fx_ref, *parts)


def later_turn(along_ref, seen_ref, count_ref, kz_ref, kf_ref, fy_ref, fx_ref, *outs):
    *parts, back_ref = outs
    step = pl.program_id(0)
    views = back_ref.shape[0]

    @pl.when(step < views)
    def _():
        def ratio(p, spot):
            seen = halves(seen_ref[0, :, spot].astype(jnp.float32))
            return (seen + damping) / below(along_ref.at[0], count_ref, kz_ref[0], spot)

        depth(ratio, kf_ref[0], back_ref, step)

    @pl.when(step >= views)
    def _():
        spread(step - views, back_ref, fy_ref, fx_ref, *parts)


def turn(args, kf, fy, fx, loads=0):
    views, ext, side = fy.shape
    planes = kf.shape[1] // 8
    chunk = 32
    folds = planes // 8
    view = lambda i: jnp.clip(i - loads, 0, views - 1)
    fold = lambda i: jnp.maximum(i - loads - views, 0)
    per_view = lambda shape: pl.BlockSpec((1,) + shape[1:], lambda i: (view(i),) + (0,) * (len(shape) - 1))
    per_fold = lambda shape: pl.BlockSpec(shape, lambda i: (fold(i), 0, 0))
    whole = lambda shape: pl.BlockSpec(shape, lambda i: (0,) * len(shape))
    shapes = [
        jax.ShapeDtypeStruct((planes, side, side), jnp.float32),
        jax.ShapeDtypeStruct((planes, 2 * PAD, side), jnp.bfloat16),
        jax.ShapeDtypeStruct((folds, ext, side), jnp.bfloat16),
        jax.ShapeDtypeStruct((folds, ext, side), jnp.bfloat16),
    ]
    out_specs = [per_fold((8, side, side)), per_fold((8, 2 * PAD, side)), per_fold((1, ext, side)), per_fold((1, ext, side))]
    filters = [per_view(kf.shape), whole(fy.shape), whole(fx.shape)]
    scratch = [pltpu.VMEM((views, planes, side, side), jnp.bfloat16)]
    if loads:
        volume = (views, planes, side, side)
        shapes.append(jax.ShapeDtypeStruct(volume, jnp.bfloat16))
        out_specs.append(per_view(volume))
        in_specs = [
            pl.BlockSpec(memory_space=pltpu.SMEM),
            pl.BlockSpec((chunk, side, side), lambda i: (jnp.minimum(i, loads - 1), 0, 0)),
            per_view(args[2].shape),
        ]
        scratch.append(pltpu.VMEM((views * planes, side, side), jnp.float32))
        kernel = functools.partial(first_turn, chunk, loads)
    else:
        in_specs = [per_view(a.shape) for a in args]
        kernel = later_turn
    return pl.pallas_call(
        kernel,
        out_shape=shapes,
        grid=(loads + views + folds,),
        in_specs=in_specs + filters,
        out_specs=out_specs,
        scratch_shapes=scratch,
        compiler_params=pltpu.CompilerParams(vmem_limit_bytes=VMEM),
        name="turn",
    )(*args, kf, fy, fx)


NEAR = [(-1, 0), (1, 0), (0, -1), (0, 1), (-1, -1), (1, -1), (-1, 1), (1, 1)]


def inside(grid, dy, dx):
    ny, nx = grid
    y = lax.axis_index("gy") + dy
    x = lax.axis_index("gx") + dx
    return (y >= 0) & (y < ny) & (x >= 0) & (x < nx), (y, x)


def greet(grid):
    barrier = pltpu.get_barrier_semaphore()
    for dy, dx in NEAR:
        there, where = inside(grid, dy, dx)

        @pl.when(there)
        def _():
            pl.semaphore_signal(barrier, inc=1, device_id=where, device_id_type=pl.DeviceIdType.MESH)

    ny, nx = grid
    y, x = lax.axis_index("gy"), lax.axis_index("gx")
    tall = 3 - (y == 0).astype(jnp.int32) - (y == ny - 1).astype(jnp.int32)
    broad = 3 - (x == 0).astype(jnp.int32) - (x == nx - 1).astype(jnp.int32)
    pl.semaphore_wait(barrier, tall * broad - 1)


def swap(grid, moves, send_sems, recv_sems):
    def copy(i, where):
        source, dest = moves[i]
        return pltpu.make_async_remote_copy(
            src_ref=source, dst_ref=dest, send_sem=send_sems.at[i], recv_sem=recv_sems.at[i],
            device_id=where, device_id_type=pl.DeviceIdType.MESH,
        )

    for i, (dy, dx) in enumerate(NEAR):
        there, where = inside(grid, dy, dx)

        @pl.when(there)
        def _():
            copy(i, where).start()

    for i, (dy, dx) in enumerate(NEAR):
        there, where = inside(grid, -dy, -dx)

        @pl.when(there)
        def _():
            copy(i, where).wait_recv()

        @pl.when(jnp.logical_not(there))
        def _():
            dest = moves[i][1]
            dest[...] = jnp.zeros(dest.shape, dest.dtype)

    for i, (dy, dx) in enumerate(NEAR):
        there, where = inside(grid, dy, dx)

        @pl.when(there)
        def _():
            copy(i, where).wait_send()


def widen(grid, fresh, wide_ref, left, right, rows, from_left, from_right, send_sems, recv_sems):
    planes, ext, _ = wide_ref.shape
    side = ext - 2 * PAD

    def cut(p, carry):
        values = []
        for k in range(8):
            plane = fresh(p * 8 + k)
            values.append(plane)
            wide_ref[p * 8 + k, :side, :side] = plane.astype(jnp.bfloat16)
        left[p] = fold_lanes(values, 0).astype(jnp.bfloat16)
        right[p] = fold_lanes(values, side - PAD).astype(jnp.bfloat16)
        return carry

    lax.fori_loop(0, planes // 8, cut, 0)
    first, last = pl.ds(0, PAD), pl.ds(side - PAD, PAD)
    whole, before, after = pl.ds(0, side), pl.ds(side, PAD), pl.ds(side + PAD, PAD)
    lanes = pl.ds(0, side)
    moves = [
        (wide_ref.at[:, first, lanes], rows.at[:, pl.ds(PAD, PAD)]),
        (wide_ref.at[:, last, lanes], rows.at[:, pl.ds(0, PAD)]),
        (left, from_right.at[:, whole]),
        (right, from_left.at[:, whole]),
        (left.at[:, first], from_right.at[:, after]),
        (left.at[:, last], from_right.at[:, before]),
        (right.at[:, first], from_left.at[:, after]),
        (right.at[:, last], from_left.at[:, before]),
    ]
    swap(grid, moves, send_sems, recv_sems)

    def paste(p, carry):
        low = from_left[p].astype(jnp.float32)
        high = from_right[p].astype(jnp.float32)
        for k in range(8):
            rim = unfold_lanes(low, k, 0) + unfold_lanes(high, k, PAD)
            wide_ref[p * 8 + k, :, side:] = rim.astype(jnp.bfloat16)
            wide_ref[p * 8 + k, side:, :side] = rows[p * 8 + k]
        return carry

    lax.fori_loop(0, planes // 8, paste, 0)


def rim_scratch(planes, side):
    ext = side + 2 * PAD
    return [
        pltpu.VMEM((planes, 2 * PAD, side), jnp.bfloat16),
        pltpu.VMEM((planes // 8, ext, side), jnp.bfloat16),
        pltpu.VMEM((planes // 8, ext, side), jnp.bfloat16),
        pltpu.SemaphoreType.DMA((8,)),
        pltpu.SemaphoreType.DMA((8,)),
    ]


def fold_scratch(planes, side):
    return [pltpu.VMEM((planes // 8, side, side), jnp.bfloat16)] * 2


def gather(grid, in_ref, ys_ref, xl_ref, xr_ref, rows, from_left, from_right, send_sems, recv_sems):
    planes, side, _ = in_ref.shape
    whole, before, after = pl.ds(0, side), pl.ds(side, PAD), pl.ds(side + PAD, PAD)
    first, second = pl.ds(0, PAD), pl.ds(PAD, PAD)
    moves = [
        (ys_ref.at[:, first], rows.at[:, second]),
        (ys_ref.at[:, second], rows.at[:, first]),
        (xl_ref.at[:, whole], from_right.at[:, whole]),
        (xr_ref.at[:, whole], from_left.at[:, whole]),
        (xl_ref.at[:, before], from_right.at[:, after]),
        (xl_ref.at[:, after], from_right.at[:, before]),
        (xr_ref.at[:, before], from_left.at[:, after]),
        (xr_ref.at[:, after], from_left.at[:, before]),
    ]
    swap(grid, moves, send_sems, recv_sems)


def totals(z, p, k, in_ref, rows, from_left, from_right):
    side = in_ref.shape[1]
    gap = jnp.zeros((side - 2 * PAD, side), jnp.float32)
    edge = rows[z].astype(jnp.float32)

    def rim(held, start):
        held = held.astype(jnp.float32)
        body = held[:side] + jnp.concatenate([held[side : side + PAD], gap, held[side + PAD :]], axis=0)
        return unfold_lanes(body, k, start)

    total = in_ref[z] + jnp.concatenate([edge[:PAD], gap, edge[PAD:]], axis=0)
    return total + rim(from_left[p], 0) + rim(from_right[p], side - PAD)


def first_kernel(grid, est_ref, wide_ref, left, right, *rim):
    greet(grid)
    widen(grid, lambda z: est_ref[z], wide_ref, left, right, *rim)


def between_kernel(grid, views, est_ref, in_ref, ys_ref, xl_ref, xr_ref, new_ref, wide_ref, *scratch):
    greet(grid)
    rim, (left, right), again = scratch[:5], scratch[5:7], scratch[7:]
    gather(grid, in_ref, ys_ref, xl_ref, xr_ref, *rim)

    def update(p, carry):
        for k in range(8):
            z = p * 8 + k
            new_ref[z] = est_ref[z] * totals(z, p, k, in_ref, *rim[:3]) / views
        return carry

    lax.fori_loop(0, est_ref.shape[0] // 8, update, 0)
    widen(grid, lambda z: new_ref[z], wide_ref, left, right, *again)


def last_kernel(grid, views, est_ref, in_ref, ys_ref, xl_ref, xr_ref, out_ref, *rim):
    greet(grid)
    gather(grid, in_ref, ys_ref, xl_ref, xr_ref, *rim)

    def update(p, carry):
        for k in range(8):
            z = p * 8 + k
            out_ref[z] = est_ref[z] * totals(z, p, k, in_ref, *rim[:3]) / views
        return carry

    lax.fori_loop(0, in_ref.shape[0] // 8, update, 0)


def rim_call(kernel, name, number, shapes, scratch, args):
    held = pl.BlockSpec(memory_space=pltpu.VMEM)
    return pl.pallas_call(
        kernel,
        out_shape=shapes,
        in_specs=[held] * len(args),
        out_specs=[held] * len(shapes),
        scratch_shapes=scratch,
        compiler_params=pltpu.CompilerParams(
            vmem_limit_bytes=VMEM, collective_id=number, has_side_effects=True
        ),
        name=name,
    )(*args)


def local(tiles, tile_dest, tile_slot, psf, estimate):
    devices = lax.axis_size("gy") * lax.axis_size("gx")
    holding, side, _ = tiles.shape
    slot_count = 2 * ((holding + devices - 1) // devices)
    views, _, taps = psf.shape
    planes = estimate.shape[0]
    target = tile_dest[:, 0]
    earlier = (target[None, :] == target[:, None]) & (
        jnp.arange(holding)[None, :] < jnp.arange(holding)[:, None]
    )
    rank = jnp.sum(earlier.astype(jnp.int32), axis=1)
    where_to = target * slot_count + rank
    placing = where_to[None, :] == jnp.arange(devices * slot_count)[:, None]
    pick = jnp.sum(jnp.where(placing, jnp.arange(holding, dtype=jnp.int32)[None, :], 0), axis=1)
    labels = jnp.sum(jnp.where(placing, tile_slot[None, :] + 1, 0), axis=1) - 1
    packed = pack(pick, tiles)
    exchange = functools.partial(
        lax.all_to_all, axis_name=("gy", "gx"), split_axis=0, concat_axis=0, tiled=True
    )
    got_labels = exchange(labels.reshape(devices, slot_count)).reshape(-1)
    grid = (lax.axis_size("gy"), lax.axis_size("gx"))
    volume = jax.ShapeDtypeStruct(estimate.shape, jnp.float32)
    framed = jax.ShapeDtypeStruct((planes, side + 2 * PAD, 2 * side), jnp.bfloat16)
    rim, folds = rim_scratch(planes, side), fold_scratch(planes, side)
    (wide,) = rim_call(functools.partial(first_kernel, grid), "rim_first", 0, [framed], folds + rim, [estimate])
    packed, wide, got_labels = lax.optimization_barrier((packed, wide, got_labels))
    got_tiles = exchange(packed.reshape(devices, slot_count, side, side)).reshape(-1, side, side)

    kernel = (psf / jnp.sum(psf, axis=2, keepdims=True)).astype(jnp.bfloat16).astype(jnp.float32)
    bx, by, kz, kf, fy, fx = bands(kernel.reshape(views * 3, taps), planes, side)

    sorting = got_labels[None, :] == jnp.arange(views * planes)[:, None]
    counted = jnp.sum(sorting.astype(jnp.float32), axis=1).reshape(views, planes)
    count = jnp.broadcast_to(counted[:, :, None], (views, planes, side))
    seen = None
    for repeat_index in range(ITERS):
        along = sides(wide, bx, by)
        if seen is None:
            weight = weigh(along, count, kz)
            *parts, seen = turn([got_labels, got_tiles, weight], kf, fy, fx, got_tiles.shape[0] // 32)
        else:
            parts = turn([along, seen, count, kz], kf, fy, fx)
        if repeat_index + 1 < ITERS:
            estimate, wide = rim_call(
                functools.partial(between_kernel, grid, views), "rim_between", 1,
                [volume, framed], rim + folds + rim, [estimate, *parts],
            )
        else:
            (estimate,) = rim_call(
                functools.partial(last_kernel, grid, views), "rim_last", 2, [volume], rim, [estimate, *parts]
            )
    return estimate


def solution(mesh):
    placed = (
        P(("gy", "gx"), None, None),
        P(("gy", "gx"), None),
        P(("gy", "gx")),
        P(),
        P(None, "gy", "gx"),
    )
    return jax.shard_map(
        local, mesh=mesh, in_specs=placed, out_specs=P(None, "gy", "gx"), check_vma=False
    )
```

```python
import functools

import jax
import jax.numpy as jnp
from jax import lax
from jax.experimental import pallas as pl
from jax.experimental.pallas import tpu as pltpu
from jax.sharding import PartitionSpec as P

ITERS = 2
PAD = 16
VMEM = 56 * 1024 * 1024

damping = 0.05


def coordinate(index, side):
    return jnp.where(index < side, index, jnp.where(index < side + PAD, index - side - PAD, index - PAD))


def toeplitz(taps_ref, row, offset):
    def add(t, held):
        return jnp.where(offset == t, taps_ref[row, t], held)

    return lax.fori_loop(0, taps_ref.shape[1], add, jnp.zeros(offset.shape, jnp.float32))


def bands_kernel(reach, planes, side, taps_ref, bx_ref, by_ref, kz_ref, kf_ref, fy_ref, fx_ref):
    views = by_ref.shape[0]
    ext = side + 2 * PAD
    wide = fx_ref.shape[1]
    iota = lambda shape, dim: lax.broadcasted_iota(jnp.int32, shape, dim)
    tall_off = coordinate(iota((ext, side), 0), side) - iota((ext, side), 1) + reach
    long_ext = iota((side, wide), 1)
    long_off = coordinate(long_ext, side) - iota((side, wide), 0) + reach
    long_off = jnp.where(long_ext < ext, long_off, -1)
    lanes = 128
    z_col = iota((planes, lanes), 1)
    z_diff = z_col - iota((planes, lanes), 0)
    full = planes * 8
    spread_l = (iota((full, planes), 0) // 8 == iota((full, planes), 1)).astype(jnp.bfloat16)
    spread_r = (iota((lanes, full), 1) // 8 == iota((lanes, full), 0)).astype(jnp.bfloat16)
    same = iota((full, full), 0) % 8 == iota((full, full), 1) % 8

    def kron(row, offset):
        small = toeplitz(taps_ref, row, offset).astype(jnp.bfloat16)
        right = jnp.dot(small, spread_r, preferred_element_type=jnp.float32).astype(jnp.bfloat16)
        both = jnp.dot(spread_l, right, preferred_element_type=jnp.float32)
        return jnp.where(same, both, 0.0).astype(jnp.bfloat16)

    for v in range(views):
        kz_ref[v] = kron(3 * v, jnp.where(z_col < planes, z_diff + reach, -1))
        kf_ref[v] = kron(3 * v, jnp.where(z_col < planes, reach - z_diff, -1))
        tall_y = toeplitz(taps_ref, 3 * v + 1, tall_off)
        long_y = toeplitz(taps_ref, 3 * v + 1, long_off)
        fy_ref[v] = tall_y.astype(jnp.bfloat16)
        by_ref[v] = long_y[:, :ext].astype(jnp.bfloat16)
        tall_x = toeplitz(taps_ref, 3 * v + 2, tall_off)
        long_x = toeplitz(taps_ref, 3 * v + 2, long_off)
        bx_ref[:ext, v * side : (v + 1) * side] = tall_x.astype(jnp.bfloat16)
        bx_ref[ext:, v * side : (v + 1) * side] = jnp.zeros((wide - ext, side), jnp.bfloat16)
        fx_ref[v * side : (v + 1) * side, :] = long_x.astype(jnp.bfloat16)


def bands(taps, planes, side):
    views = taps.shape[0] // 3
    ext = side + 2 * PAD
    shapes = [
        (2 * side, views * side),
        (views, side, ext),
        (views, planes * 8, planes * 8),
        (views, planes * 8, planes * 8),
        (views, ext, side),
        (views * side, 2 * side),
    ]
    return pl.pallas_call(
        functools.partial(bands_kernel, (taps.shape[1] - 1) // 2, planes, side),
        out_shape=[jax.ShapeDtypeStruct(s, jnp.bfloat16) for s in shapes],
        in_specs=[pl.BlockSpec(memory_space=pltpu.SMEM)],
        out_specs=[pl.BlockSpec(memory_space=pltpu.VMEM)] * len(shapes),
        compiler_params=pltpu.CompilerParams(vmem_limit_bytes=VMEM),
        name="bands",
    )(taps)


def pack_kernel(pick_ref, tiles_ref, out_ref, sem):
    count = out_ref.shape[0]

    def send(slot, carry):
        pltpu.make_async_copy(tiles_ref.at[pick_ref[slot]], out_ref.at[slot], sem).start()
        return carry

    lax.fori_loop(0, count, send, 0)
    pltpu.make_async_copy(out_ref, out_ref, sem).wait()


def pack(pick, tiles):
    count = pick.shape[0]
    return pl.pallas_call(
        pack_kernel,
        out_shape=jax.ShapeDtypeStruct((count,) + tiles.shape[1:], tiles.dtype),
        in_specs=[pl.BlockSpec(memory_space=pltpu.SMEM), pl.BlockSpec(memory_space=pltpu.VMEM)],
        out_specs=pl.BlockSpec(memory_space=pl.ANY),
        scratch_shapes=[pltpu.SemaphoreType.DMA],
        compiler_params=pltpu.CompilerParams(vmem_limit_bytes=VMEM),
        name="pack",
    )(pick, tiles)


def sides_kernel(wide_ref, bx_ref, by_ref, out_ref):
    views, planes, side, _ = out_ref.shape
    along_y = [
        jnp.dot(by_ref[...], wide_ref[z], preferred_element_type=jnp.float32).astype(jnp.bfloat16)
        for z in range(planes)
    ]
    for v in range(views):
        spot = slice(v * side, (v + 1) * side)
        stack = jnp.concatenate([one[spot] for one in along_y], axis=0)
        both = jnp.dot(stack, bx_ref[:, spot], preferred_element_type=jnp.float32)
        out_ref[v] = both.astype(jnp.bfloat16).reshape(planes, side, side)


def sides(wide, bx, by):
    planes, ext, _ = wide.shape
    views, side, _ = by.shape
    by = by.reshape(views * side, ext)
    chunk = 4
    macs = planes * ext * ext * side * views + planes * views * side * side * ext
    return pl.pallas_call(
        sides_kernel,
        out_shape=jax.ShapeDtypeStruct((views, planes, side, side), jnp.bfloat16),
        grid=(planes // chunk,),
        in_specs=[
            pl.BlockSpec((chunk,) + wide.shape[1:], lambda i: (i, 0, 0)),
            pl.BlockSpec(bx.shape, lambda i: (0, 0)),
            pl.BlockSpec(by.shape, lambda i: (0, 0)),
        ],
        out_specs=pl.BlockSpec((views, chunk, side, side), lambda i: (0, i, 0, 0)),
        compiler_params=pltpu.CompilerParams(vmem_limit_bytes=VMEM),
        cost_estimate=pl.CostEstimate(flops=2 * macs, bytes_accessed=views * planes * side * side * 3, transcendentals=0),
        name="sides",
    )(wide, bx, by)


def halves(values):
    planes, _, side = values.shape
    full = planes * 8
    return jnp.concatenate([values[:, :8].reshape(full, side), values[:, 8:].reshape(full, side)], axis=1)


def below(along, count_ref, kz, spot):
    planes, side, _ = along.shape
    full = planes * 8
    count = jnp.broadcast_to(count_ref[0][:, None, :], (planes, 8, side)).reshape(full, side)
    stack = halves(along[:, spot].astype(jnp.float32)).astype(jnp.bfloat16)
    blur = jnp.dot(kz, stack, preferred_element_type=jnp.float32)
    return jnp.concatenate([count, count], axis=1) * blur + damping


def weigh_kernel(along_ref, count_ref, kz_ref, out_ref):
    for p in range(out_ref.shape[1]):
        out_ref[0, p] = 1.0 / below(along_ref.at[0], count_ref, kz_ref[0], slice(p * 16, p * 16 + 16))


def weigh(along, count, kz):
    views, planes, side, _ = along.shape
    pairs, full = side // 16, planes * 8
    per_view = lambda shape: pl.BlockSpec((1,) + shape[1:], lambda i: (i,) + (0,) * (len(shape) - 1))
    shape = (views, pairs, full, 2 * side)
    return pl.pallas_call(
        weigh_kernel,
        out_shape=jax.ShapeDtypeStruct(shape, jnp.float32),
        grid=(views,),
        in_specs=[per_view(along.shape), per_view(count.shape), per_view(kz.shape)],
        out_specs=per_view(shape),
        compiler_params=pltpu.CompilerParams(vmem_limit_bytes=VMEM),
        name="weigh",
    )(along, count, kz)


def depth(ratio, kf, back_ref, v):
    _, planes, side, _ = back_ref.shape
    for p in range(side // 16):
        spot = slice(p * 16, p * 16 + 16)
        back = jnp.dot(kf, ratio(p, spot).astype(jnp.bfloat16), preferred_element_type=jnp.float32)
        back_ref[v, :, spot] = jnp.concatenate(
            [back[:, :side].reshape(planes, 8, side), back[:, side:].reshape(planes, 8, side)], axis=1
        ).astype(jnp.bfloat16)


def fold_lanes(values, start):
    lane = lax.broadcasted_iota(jnp.int32, values[0].shape, 1)
    held = jnp.zeros(values[0].shape, jnp.float32)
    for k, one in enumerate(values):
        held = jnp.where(lane // PAD == k, pltpu.roll(one, (PAD * k - start) % 128, 1), held)
    return held


def unfold_lanes(held, k, start):
    lane = lax.broadcasted_iota(jnp.int32, held.shape, 1)
    return jnp.where(lane // PAD == start // PAD, pltpu.roll(held, (start - PAD * k) % 128, 1), 0.0)


def spread(fold, back_ref, fy_ref, fx_ref, in_ref, ys_ref, xl_ref, xr_ref):
    views, _, side, _ = back_ref.shape
    rims = []
    for z in range(8):
        wide = jnp.concatenate(
            [
                jnp.dot(fy_ref[v], back_ref[v, fold * 8 + z], preferred_element_type=jnp.float32).astype(jnp.bfloat16)
                for v in range(views)
            ],
            axis=1,
        )
        part = jnp.dot(wide, fx_ref[...], preferred_element_type=jnp.float32)
        in_ref[z] = part[:side, :side]
        ys_ref[z] = part[side:, :side].astype(jnp.bfloat16)
        rims.append(part[:, side:])
    xl_ref[0] = fold_lanes(rims, 0).astype(jnp.bfloat16)
    xr_ref[0] = fold_lanes(rims, PAD).astype(jnp.bfloat16)


def first_turn(chunk, loads, label_ref, tiles_ref, weight_ref, kf_ref, fy_ref, fx_ref, *outs):
    *parts, seen_ref, back_ref, held_ref = outs
    step = pl.program_id(0)
    views, planes = back_ref.shape[:2]

    @pl.when(step == 0)
    def _():
        def clear(plane, carry):
            held_ref[plane] = jnp.zeros(held_ref.shape[1:], jnp.float32)
            return carry

        lax.fori_loop(0, views * planes + 1, clear, 0)

    @pl.when(step < loads)
    def _():
        def add(i, carry):
            label = label_ref[step * chunk + i]
            spot = jnp.where(label < 0, views * planes, label)
            held_ref[spot] += tiles_ref[i].astype(jnp.float32)
            return carry

        lax.fori_loop(0, chunk, add, 0, unroll=4)

    @pl.when((step >= loads) & (step < loads + views))
    def _():
        v = step - loads
        base = pl.multiple_of(v * planes, planes)

        def ratio(p, spot):
            seen = held_ref[pl.ds(base, planes), spot]
            seen_ref[0, :, spot] = seen.astype(jnp.bfloat16)
            return (halves(seen) + damping) * weight_ref[0, p]

        depth(ratio, kf_ref[0], back_ref, v)

    @pl.when(step >= loads + views)
    def _():
        spread(step - loads - views, back_ref, fy_ref, fx_ref, *parts)


def later_turn(along_ref, seen_ref, count_ref, kz_ref, kf_ref, fy_ref, fx_ref, *outs):
    *parts, back_ref = outs
    step = pl.program_id(0)
    views = back_ref.shape[0]

    @pl.when(step < views)
    def _():
        def ratio(p, spot):
            seen = halves(seen_ref[0, :, spot].astype(jnp.float32))
            return (seen + damping) / below(along_ref.at[0], count_ref, kz_ref[0], spot)

        depth(ratio, kf_ref[0], back_ref, step)

    @pl.when(step >= views)
    def _():
        spread(step - views, back_ref, fy_ref, fx_ref, *parts)


def turn(args, kf, fy, fx, loads=0):
    views, ext, side = fy.shape
    planes = kf.shape[1] // 8
    chunk = 32
    folds = planes // 8
    view = lambda i: jnp.clip(i - loads, 0, views - 1)
    fold = lambda i: jnp.maximum(i - loads - views, 0)
    per_view = lambda shape: pl.BlockSpec((1,) + shape[1:], lambda i: (view(i),) + (0,) * (len(shape) - 1))
    per_fold = lambda shape: pl.BlockSpec(shape, lambda i: (fold(i), 0, 0))
    whole = lambda shape: pl.BlockSpec(shape, lambda i: (0,) * len(shape))
    shapes = [
        jax.ShapeDtypeStruct((planes, side, side), jnp.float32),
        jax.ShapeDtypeStruct((planes, 2 * PAD, side), jnp.bfloat16),
        jax.ShapeDtypeStruct((folds, ext, side), jnp.bfloat16),
        jax.ShapeDtypeStruct((folds, ext, side), jnp.bfloat16),
    ]
    out_specs = [per_fold((8, side, side)), per_fold((8, 2 * PAD, side)), per_fold((1, ext, side)), per_fold((1, ext, side))]
    filters = [per_view(kf.shape), whole(fy.shape), whole(fx.shape)]
    scratch = [pltpu.VMEM((views, planes, side, side), jnp.bfloat16)]
    if loads:
        volume = (views, planes, side, side)
        shapes.append(jax.ShapeDtypeStruct(volume, jnp.bfloat16))
        out_specs.append(per_view(volume))
        in_specs = [
            pl.BlockSpec(memory_space=pltpu.SMEM),
            pl.BlockSpec((chunk, side, side), lambda i: (jnp.minimum(i, loads - 1), 0, 0)),
            per_view(args[2].shape),
        ]
        scratch.append(pltpu.VMEM((views * planes + 1, side, side), jnp.float32))
        kernel = functools.partial(first_turn, chunk, loads)
    else:
        in_specs = [per_view(a.shape) for a in args]
        kernel = later_turn
    return pl.pallas_call(
        kernel,
        out_shape=shapes,
        grid=(loads + views + folds,),
        in_specs=in_specs + filters,
        out_specs=out_specs,
        scratch_shapes=scratch,
        compiler_params=pltpu.CompilerParams(vmem_limit_bytes=VMEM),
        name="turn",
    )(*args, kf, fy, fx)


NEAR = [(-1, 0), (1, 0), (0, -1), (0, 1), (-1, -1), (1, -1), (-1, 1), (1, 1)]


def inside(grid, dy, dx):
    ny, nx = grid
    y = lax.axis_index("gy") + dy
    x = lax.axis_index("gx") + dx
    return (y >= 0) & (y < ny) & (x >= 0) & (x < nx), (y, x)


def greet(grid):
    barrier = pltpu.get_barrier_semaphore()
    for dy, dx in NEAR:
        there, where = inside(grid, dy, dx)

        @pl.when(there)
        def _():
            pl.semaphore_signal(barrier, inc=1, device_id=where, device_id_type=pl.DeviceIdType.MESH)

    ny, nx = grid
    y, x = lax.axis_index("gy"), lax.axis_index("gx")
    tall = 3 - (y == 0).astype(jnp.int32) - (y == ny - 1).astype(jnp.int32)
    broad = 3 - (x == 0).astype(jnp.int32) - (x == nx - 1).astype(jnp.int32)
    pl.semaphore_wait(barrier, tall * broad - 1)


def move(i, where, moves, send_sems, recv_sems):
    source, dest = moves[i]
    return pltpu.make_async_remote_copy(
        src_ref=source, dst_ref=dest, send_sem=send_sems.at[i], recv_sem=recv_sems.at[i],
        device_id=where, device_id_type=pl.DeviceIdType.MESH,
    )


def launch(grid, which, moves, send_sems, recv_sems):
    for i in which:
        there, where = inside(grid, *NEAR[i])

        @pl.when(there)
        def _():
            move(i, where, moves, send_sems, recv_sems).start()


def land(grid, moves, send_sems, recv_sems):
    for i, (dy, dx) in enumerate(NEAR):
        there, where = inside(grid, -dy, -dx)

        @pl.when(there)
        def _():
            move(i, where, moves, send_sems, recv_sems).wait_recv()

        @pl.when(jnp.logical_not(there))
        def _():
            dest = moves[i][1]
            dest[...] = jnp.zeros(dest.shape, dest.dtype)

    for i, (dy, dx) in enumerate(NEAR):
        there, where = inside(grid, dy, dx)

        @pl.when(there)
        def _():
            move(i, where, moves, send_sems, recv_sems).wait_send()


def widen(grid, fresh, wide_ref, left, right, rows, from_left, from_right, send_sems, recv_sems):
    planes, ext, _ = wide_ref.shape
    side = ext - 2 * PAD

    first, last = pl.ds(0, PAD), pl.ds(side - PAD, PAD)
    whole, before, after = pl.ds(0, side), pl.ds(side, PAD), pl.ds(side + PAD, PAD)
    lanes = pl.ds(0, side)
    moves = [
        (wide_ref.at[:, first, lanes], rows.at[:, pl.ds(PAD, PAD)]),
        (wide_ref.at[:, last, lanes], rows.at[:, pl.ds(0, PAD)]),
        (left, from_right.at[:, whole]),
        (right, from_left.at[:, whole]),
        (left.at[:, first], from_right.at[:, after]),
        (left.at[:, last], from_right.at[:, before]),
        (right.at[:, first], from_left.at[:, after]),
        (right.at[:, last], from_left.at[:, before]),
    ]

    def cast(z, carry):
        wide_ref[z, :side, :side] = fresh(z).astype(jnp.bfloat16)
        return carry

    lax.fori_loop(0, planes, cast, 0, unroll=4)
    launch(grid, (0, 1), moves, send_sems, recv_sems)

    def cut(p, carry):
        values = [fresh(p * 8 + k) for k in range(8)]
        left[p] = fold_lanes(values, 0).astype(jnp.bfloat16)
        right[p] = fold_lanes(values, side - PAD).astype(jnp.bfloat16)
        return carry

    lax.fori_loop(0, planes // 8, cut, 0)
    launch(grid, range(2, 8), moves, send_sems, recv_sems)
    land(grid, moves, send_sems, recv_sems)

    def paste(p, carry):
        low = from_left[p].astype(jnp.float32)
        high = from_right[p].astype(jnp.float32)
        for k in range(8):
            rim = unfold_lanes(low, k, 0) + unfold_lanes(high, k, PAD)
            wide_ref[p * 8 + k, :, side:] = rim.astype(jnp.bfloat16)
            wide_ref[p * 8 + k, side:, :side] = rows[p * 8 + k]
        return carry

    lax.fori_loop(0, planes // 8, paste, 0)


def rim_scratch(planes, side):
    ext = side + 2 * PAD
    return [
        pltpu.VMEM((planes, 2 * PAD, side), jnp.bfloat16),
        pltpu.VMEM((planes // 8, ext, side), jnp.bfloat16),
        pltpu.VMEM((planes // 8, ext, side), jnp.bfloat16),
        pltpu.SemaphoreType.DMA((8,)),
        pltpu.SemaphoreType.DMA((8,)),
    ]


def fold_scratch(planes, side):
    return [pltpu.VMEM((planes // 8, side, side), jnp.bfloat16)] * 2


def gather(grid, in_ref, ys_ref, xl_ref, xr_ref, rows, from_left, from_right, send_sems, recv_sems):
    planes, side, _ = in_ref.shape
    whole, before, after = pl.ds(0, side), pl.ds(side, PAD), pl.ds(side + PAD, PAD)
    first, second = pl.ds(0, PAD), pl.ds(PAD, PAD)
    moves = [
        (ys_ref.at[:, first], rows.at[:, second]),
        (ys_ref.at[:, second], rows.at[:, first]),
        (xl_ref.at[:, whole], from_right.at[:, whole]),
        (xr_ref.at[:, whole], from_left.at[:, whole]),
        (xl_ref.at[:, before], from_right.at[:, after]),
        (xl_ref.at[:, after], from_right.at[:, before]),
        (xr_ref.at[:, before], from_left.at[:, after]),
        (xr_ref.at[:, after], from_left.at[:, before]),
    ]
    launch(grid, range(8), moves, send_sems, recv_sems)
    land(grid, moves, send_sems, recv_sems)


def totals(z, p, k, in_ref, rows, from_left, from_right):
    side = in_ref.shape[1]
    gap = jnp.zeros((side - 2 * PAD, side), jnp.float32)
    edge = rows[z].astype(jnp.float32)

    def rim(held, start):
        held = held.astype(jnp.float32)
        body = held[:side] + jnp.concatenate([held[side : side + PAD], gap, held[side + PAD :]], axis=0)
        return unfold_lanes(body, k, start)

    total = in_ref[z] + jnp.concatenate([edge[:PAD], gap, edge[PAD:]], axis=0)
    return total + rim(from_left[p], 0) + rim(from_right[p], side - PAD)


def first_kernel(grid, est_ref, wide_ref, left, right, *rim):
    greet(grid)
    widen(grid, lambda z: est_ref[z], wide_ref, left, right, *rim)


def between_kernel(grid, views, est_ref, in_ref, ys_ref, xl_ref, xr_ref, new_ref, wide_ref, *scratch):
    greet(grid)
    rim, (left, right), again = scratch[:5], scratch[5:7], scratch[7:]
    gather(grid, in_ref, ys_ref, xl_ref, xr_ref, *rim)

    def update(p, carry):
        for k in range(8):
            z = p * 8 + k
            new_ref[z] = est_ref[z] * totals(z, p, k, in_ref, *rim[:3]) / views
        return carry

    lax.fori_loop(0, est_ref.shape[0] // 8, update, 0)
    widen(grid, lambda z: new_ref[z], wide_ref, left, right, *again)


def last_kernel(grid, views, est_ref, in_ref, ys_ref, xl_ref, xr_ref, out_ref, *rim):
    greet(grid)
    gather(grid, in_ref, ys_ref, xl_ref, xr_ref, *rim)

    def update(p, carry):
        for k in range(8):
            z = p * 8 + k
            out_ref[z] = est_ref[z] * totals(z, p, k, in_ref, *rim[:3]) / views
        return carry

    lax.fori_loop(0, in_ref.shape[0] // 8, update, 0)


def rim_call(kernel, name, number, shapes, scratch, args):
    held = pl.BlockSpec(memory_space=pltpu.VMEM)
    return pl.pallas_call(
        kernel,
        out_shape=shapes,
        in_specs=[held] * len(args),
        out_specs=[held] * len(shapes),
        scratch_shapes=scratch,
        compiler_params=pltpu.CompilerParams(
            vmem_limit_bytes=VMEM, collective_id=number, has_side_effects=True
        ),
        name=name,
    )(*args)


def local(tiles, tile_dest, tile_slot, psf, estimate):
    devices = lax.axis_size("gy") * lax.axis_size("gx")
    holding, side, _ = tiles.shape
    slot_count = 2 * ((holding + devices - 1) // devices)
    views, _, taps = psf.shape
    planes = estimate.shape[0]
    target = tile_dest[:, 0]
    earlier = (target[None, :] == target[:, None]) & (
        jnp.arange(holding)[None, :] < jnp.arange(holding)[:, None]
    )
    rank = jnp.sum(earlier.astype(jnp.int32), axis=1)
    where_to = target * slot_count + rank
    placing = where_to[None, :] == jnp.arange(devices * slot_count)[:, None]
    pick = jnp.sum(jnp.where(placing, jnp.arange(holding, dtype=jnp.int32)[None, :], 0), axis=1)
    labels = jnp.sum(jnp.where(placing, tile_slot[None, :] + 1, 0), axis=1) - 1
    packed = pack(pick, tiles)
    exchange = functools.partial(
        lax.all_to_all, axis_name=("gy", "gx"), split_axis=0, concat_axis=0, tiled=True
    )
    got_labels = exchange(labels.reshape(devices, slot_count)).reshape(-1)
    grid = (lax.axis_size("gy"), lax.axis_size("gx"))
    volume = jax.ShapeDtypeStruct(estimate.shape, jnp.float32)
    framed = jax.ShapeDtypeStruct((planes, side + 2 * PAD, 2 * side), jnp.bfloat16)
    rim, folds = rim_scratch(planes, side), fold_scratch(planes, side)
    packed, psf, got_labels = lax.optimization_barrier((packed, psf, got_labels))
    got_tiles = exchange(packed.reshape(devices, slot_count, side, side)).reshape(-1, side, side)

    kernel = (psf / jnp.sum(psf, axis=2, keepdims=True)).astype(jnp.bfloat16).astype(jnp.float32)
    bx, by, kz, kf, fy, fx = bands(kernel.reshape(views * 3, taps), planes, side)

    bx, start = lax.optimization_barrier((bx, estimate))
    (wide,) = rim_call(functools.partial(first_kernel, grid), "rim_first", 0, [framed], folds + rim, [start])

    sorting = got_labels[None, :] == jnp.arange(views * planes)[:, None]
    counted = jnp.sum(sorting.astype(jnp.float32), axis=1).reshape(views, planes)
    count = jnp.broadcast_to(counted[:, :, None], (views, planes, side))
    seen = None
    for repeat_index in range(ITERS):
        along = sides(wide, bx, by)
        if seen is None:
            weight = weigh(along, count, kz)
            *parts, seen = turn([got_labels, got_tiles, weight], kf, fy, fx, got_tiles.shape[0] // 32)
        else:
            parts = turn([along, seen, count, kz], kf, fy, fx)
        if repeat_index + 1 < ITERS:
            estimate, wide = rim_call(
                functools.partial(between_kernel, grid, views), "rim_between", 1,
                [volume, framed], rim + folds + rim, [estimate, *parts],
            )
        else:
            (estimate,) = rim_call(
                functools.partial(last_kernel, grid, views), "rim_last", 2, [volume], rim, [estimate, *parts]
            )
    return estimate


def solution(mesh):
    placed = (
        P(("gy", "gx"), None, None),
        P(("gy", "gx"), None),
        P(("gy", "gx")),
        P(),
        P(None, "gy", "gx"),
    )
    return jax.shard_map(
        local, mesh=mesh, in_specs=placed, out_specs=P(None, "gy", "gx"), check_vma=False
    )
```

```python
import functools

import jax
import jax.numpy as jnp
from jax import lax
from jax.experimental import pallas as pl
from jax.experimental.pallas import tpu as pltpu
from jax.sharding import PartitionSpec as P

ITERS = 2
PAD = 16
VMEM = 56 * 1024 * 1024

damping = 0.05


def coordinate(index, side):
    return jnp.where(index < side, index, jnp.where(index < side + PAD, index - side - PAD, index - PAD))


def toeplitz(taps_ref, row, offset):
    def add(t, held):
        return jnp.where(offset == t, taps_ref[row, t], held)

    return lax.fori_loop(0, taps_ref.shape[1], add, jnp.zeros(offset.shape, jnp.float32))


def bands_kernel(reach, planes, side, taps_ref, bx_ref, by_ref, kz_ref, kf_ref, fy_ref, fx_ref):
    views = by_ref.shape[0]
    ext = side + 2 * PAD
    wide = fx_ref.shape[1]
    iota = lambda shape, dim: lax.broadcasted_iota(jnp.int32, shape, dim)
    tall_off = coordinate(iota((ext, side), 0), side) - iota((ext, side), 1) + reach
    long_ext = iota((side, wide), 1)
    long_off = coordinate(long_ext, side) - iota((side, wide), 0) + reach
    long_off = jnp.where(long_ext < ext, long_off, -1)
    lanes = 128
    z_col = iota((planes, lanes), 1)
    z_diff = z_col - iota((planes, lanes), 0)
    full = planes * 8
    spread_l = (iota((full, planes), 0) // 8 == iota((full, planes), 1)).astype(jnp.bfloat16)
    spread_r = (iota((lanes, full), 1) // 8 == iota((lanes, full), 0)).astype(jnp.bfloat16)
    same = iota((full, full), 0) % 8 == iota((full, full), 1) % 8

    def kron(row, offset):
        small = toeplitz(taps_ref, row, offset).astype(jnp.bfloat16)
        right = jnp.dot(small, spread_r, preferred_element_type=jnp.float32).astype(jnp.bfloat16)
        both = jnp.dot(spread_l, right, preferred_element_type=jnp.float32)
        return jnp.where(same, both, 0.0).astype(jnp.bfloat16)

    for v in range(views):
        kz_ref[v] = kron(3 * v, jnp.where(z_col < planes, z_diff + reach, -1))
        kf_ref[v] = kron(3 * v, jnp.where(z_col < planes, reach - z_diff, -1))
        tall_y = toeplitz(taps_ref, 3 * v + 1, tall_off)
        long_y = toeplitz(taps_ref, 3 * v + 1, long_off)
        fy_ref[v] = tall_y.astype(jnp.bfloat16)
        by_ref[v] = long_y[:, :ext].astype(jnp.bfloat16)
        tall_x = toeplitz(taps_ref, 3 * v + 2, tall_off)
        long_x = toeplitz(taps_ref, 3 * v + 2, long_off)
        bx_ref[:ext, v * side : (v + 1) * side] = tall_x.astype(jnp.bfloat16)
        bx_ref[ext:, v * side : (v + 1) * side] = jnp.zeros((wide - ext, side), jnp.bfloat16)
        fx_ref[v * side : (v + 1) * side, :] = long_x.astype(jnp.bfloat16)


def bands(taps, planes, side):
    views = taps.shape[0] // 3
    ext = side + 2 * PAD
    shapes = [
        (2 * side, views * side),
        (views, side, ext),
        (views, planes * 8, planes * 8),
        (views, planes * 8, planes * 8),
        (views, ext, side),
        (views * side, 2 * side),
    ]
    return pl.pallas_call(
        functools.partial(bands_kernel, (taps.shape[1] - 1) // 2, planes, side),
        out_shape=[jax.ShapeDtypeStruct(s, jnp.bfloat16) for s in shapes],
        in_specs=[pl.BlockSpec(memory_space=pltpu.SMEM)],
        out_specs=[pl.BlockSpec(memory_space=pltpu.VMEM)] * len(shapes),
        compiler_params=pltpu.CompilerParams(vmem_limit_bytes=VMEM),
        name="bands",
    )(taps)


def pack_kernel(pick_ref, tiles_ref, out_ref, sem):
    count = out_ref.shape[0]

    def send(slot, carry):
        pltpu.make_async_copy(tiles_ref.at[pick_ref[slot]], out_ref.at[slot], sem).start()
        return carry

    lax.fori_loop(0, count, send, 0)
    pltpu.make_async_copy(out_ref, out_ref, sem).wait()


def pack(pick, tiles):
    count = pick.shape[0]
    return pl.pallas_call(
        pack_kernel,
        out_shape=jax.ShapeDtypeStruct((count,) + tiles.shape[1:], tiles.dtype),
        in_specs=[pl.BlockSpec(memory_space=pltpu.SMEM), pl.BlockSpec(memory_space=pltpu.VMEM)],
        out_specs=pl.BlockSpec(memory_space=pl.ANY),
        scratch_shapes=[pltpu.SemaphoreType.DMA],
        compiler_params=pltpu.CompilerParams(vmem_limit_bytes=VMEM),
        name="pack",
    )(pick, tiles)


def sides_kernel(wide_ref, bx_ref, by_ref, out_ref):
    views, planes, side, _ = out_ref.shape
    along_y = [
        jnp.dot(by_ref[...], wide_ref[z], preferred_element_type=jnp.float32).astype(jnp.bfloat16)
        for z in range(planes)
    ]
    for v in range(views):
        spot = slice(v * side, (v + 1) * side)
        stack = jnp.concatenate([one[spot] for one in along_y], axis=0)
        both = jnp.dot(stack, bx_ref[:, spot], preferred_element_type=jnp.float32)
        out_ref[v] = both.astype(jnp.bfloat16).reshape(planes, side, side)


def sides(wide, bx, by):
    planes, ext, _ = wide.shape
    views, side, _ = by.shape
    by = by.reshape(views * side, ext)
    chunk = 4
    macs = planes * ext * ext * side * views + planes * views * side * side * ext
    return pl.pallas_call(
        sides_kernel,
        out_shape=jax.ShapeDtypeStruct((views, planes, side, side), jnp.bfloat16),
        grid=(planes // chunk,),
        in_specs=[
            pl.BlockSpec((chunk,) + wide.shape[1:], lambda i: (i, 0, 0)),
            pl.BlockSpec(bx.shape, lambda i: (0, 0)),
            pl.BlockSpec(by.shape, lambda i: (0, 0)),
        ],
        out_specs=pl.BlockSpec((views, chunk, side, side), lambda i: (0, i, 0, 0)),
        compiler_params=pltpu.CompilerParams(vmem_limit_bytes=VMEM),
        cost_estimate=pl.CostEstimate(flops=2 * macs, bytes_accessed=views * planes * side * side * 3, transcendentals=0),
        name="sides",
    )(wide, bx, by)


def halves(values):
    planes, _, side = values.shape
    full = planes * 8
    return jnp.concatenate([values[:, :8].reshape(full, side), values[:, 8:].reshape(full, side)], axis=1)


def below(along, count_ref, kz, spot):
    planes, side, _ = along.shape
    full = planes * 8
    count = jnp.broadcast_to(count_ref[0][:, None, :], (planes, 8, side)).reshape(full, side)
    stack = halves(along[:, spot].astype(jnp.float32)).astype(jnp.bfloat16)
    blur = jnp.dot(kz, stack, preferred_element_type=jnp.float32)
    return jnp.concatenate([count, count], axis=1) * blur + damping


def weigh_kernel(along_ref, count_ref, kz_ref, out_ref):
    for p in range(out_ref.shape[1]):
        out_ref[0, p] = 1.0 / below(along_ref.at[0], count_ref, kz_ref[0], slice(p * 16, p * 16 + 16))


def weigh(along, count, kz):
    views, planes, side, _ = along.shape
    pairs, full = side // 16, planes * 8
    per_view = lambda shape: pl.BlockSpec((1,) + shape[1:], lambda i: (i,) + (0,) * (len(shape) - 1))
    shape = (views, pairs, full, 2 * side)
    return pl.pallas_call(
        weigh_kernel,
        out_shape=jax.ShapeDtypeStruct(shape, jnp.float32),
        grid=(views,),
        in_specs=[per_view(along.shape), per_view(count.shape), per_view(kz.shape)],
        out_specs=per_view(shape),
        compiler_params=pltpu.CompilerParams(vmem_limit_bytes=VMEM),
        name="weigh",
    )(along, count, kz)


def depth(ratio, kf, back_ref, v):
    _, planes, side, _ = back_ref.shape
    for p in range(side // 16):
        spot = slice(p * 16, p * 16 + 16)
        back = jnp.dot(kf, ratio(p, spot).astype(jnp.bfloat16), preferred_element_type=jnp.float32)
        back_ref[v, :, spot] = jnp.concatenate(
            [back[:, :side].reshape(planes, 8, side), back[:, side:].reshape(planes, 8, side)], axis=1
        ).astype(jnp.bfloat16)


def fold_lanes(values, start):
    lane = lax.broadcasted_iota(jnp.int32, values[0].shape, 1)
    held = jnp.zeros(values[0].shape, jnp.float32)
    for k, one in enumerate(values):
        held = jnp.where(lane // PAD == k, pltpu.roll(one, (PAD * k - start) % 128, 1), held)
    return held


def unfold_lanes(held, k, start):
    lane = lax.broadcasted_iota(jnp.int32, held.shape, 1)
    return jnp.where(lane // PAD == start // PAD, pltpu.roll(held, (start - PAD * k) % 128, 1), 0.0)


def spread(fold, back_ref, fy_ref, fx_ref, in_ref, ys_ref, xl_ref, xr_ref):
    views, _, side, _ = back_ref.shape
    rims = []
    for z in range(8):
        wide = jnp.concatenate(
            [
                jnp.dot(fy_ref[v], back_ref[v, fold * 8 + z], preferred_element_type=jnp.float32).astype(jnp.bfloat16)
                for v in range(views)
            ],
            axis=1,
        )
        part = jnp.dot(wide, fx_ref[...], preferred_element_type=jnp.float32)
        in_ref[z] = part[:side, :side]
        ys_ref[z] = part[side:, :side].astype(jnp.bfloat16)
        rims.append(part[:, side:])
    xl_ref[0] = fold_lanes(rims, 0).astype(jnp.bfloat16)
    xr_ref[0] = fold_lanes(rims, PAD).astype(jnp.bfloat16)


def first_turn(chunk, loads, label_ref, tiles_ref, weight_ref, kf_ref, fy_ref, fx_ref, *outs):
    *parts, seen_ref, back_ref, held_ref = outs
    step = pl.program_id(0)
    views, planes = back_ref.shape[:2]

    @pl.when(step == 0)
    def _():
        def clear(plane, carry):
            held_ref[plane] = jnp.zeros(held_ref.shape[1:], jnp.float32)
            return carry

        lax.fori_loop(0, views * planes + 1, clear, 0)

    @pl.when(step < loads)
    def _():
        def add(i, carry):
            label = label_ref[step * chunk + i]
            spot = jnp.where(label < 0, views * planes, label)
            held_ref[spot] += tiles_ref[i].astype(jnp.float32)
            return carry

        lax.fori_loop(0, chunk, add, 0, unroll=4)

    @pl.when((step >= loads) & (step < loads + views))
    def _():
        v = step - loads
        base = pl.multiple_of(v * planes, planes)

        def ratio(p, spot):
            seen = held_ref[pl.ds(base, planes), spot]
            seen_ref[0, :, spot] = seen.astype(jnp.bfloat16)
            return (halves(seen) + damping) * weight_ref[0, p]

        depth(ratio, kf_ref[0], back_ref, v)

    @pl.when(step >= loads + views)
    def _():
        spread(step - loads - views, back_ref, fy_ref, fx_ref, *parts)


def later_turn(along_ref, seen_ref, count_ref, kz_ref, kf_ref, fy_ref, fx_ref, *outs):
    *parts, back_ref = outs
    step = pl.program_id(0)
    views = back_ref.shape[0]

    @pl.when(step < views)
    def _():
        def ratio(p, spot):
            seen = halves(seen_ref[0, :, spot].astype(jnp.float32))
            return (seen + damping) / below(along_ref.at[0], count_ref, kz_ref[0], spot)

        depth(ratio, kf_ref[0], back_ref, step)

    @pl.when(step >= views)
    def _():
        spread(step - views, back_ref, fy_ref, fx_ref, *parts)


def turn(args, kf, fy, fx, loads=0):
    views, ext, side = fy.shape
    planes = kf.shape[1] // 8
    chunk = 32
    folds = planes // 8
    view = lambda i: jnp.clip(i - loads, 0, views - 1)
    fold = lambda i: jnp.maximum(i - loads - views, 0)
    per_view = lambda shape: pl.BlockSpec((1,) + shape[1:], lambda i: (view(i),) + (0,) * (len(shape) - 1))
    per_fold = lambda shape: pl.BlockSpec(shape, lambda i: (fold(i), 0, 0))
    whole = lambda shape: pl.BlockSpec(shape, lambda i: (0,) * len(shape))
    shapes = [
        jax.ShapeDtypeStruct((planes, side, side), jnp.float32),
        jax.ShapeDtypeStruct((planes, 2 * PAD, side), jnp.bfloat16),
        jax.ShapeDtypeStruct((folds, ext, side), jnp.bfloat16),
        jax.ShapeDtypeStruct((folds, ext, side), jnp.bfloat16),
    ]
    out_specs = [per_fold((8, side, side)), per_fold((8, 2 * PAD, side)), per_fold((1, ext, side)), per_fold((1, ext, side))]
    filters = [per_view(kf.shape), whole(fy.shape), whole(fx.shape)]
    scratch = [pltpu.VMEM((views, planes, side, side), jnp.bfloat16)]
    if loads:
        volume = (views, planes, side, side)
        shapes.append(jax.ShapeDtypeStruct(volume, jnp.bfloat16))
        out_specs.append(per_view(volume))
        in_specs = [
            pl.BlockSpec(memory_space=pltpu.SMEM),
            pl.BlockSpec((chunk, side, side), lambda i: (jnp.minimum(i, loads - 1), 0, 0)),
            per_view(args[2].shape),
        ]
        scratch.append(pltpu.VMEM((views * planes + 1, side, side), jnp.float32))
        kernel = functools.partial(first_turn, chunk, loads)
    else:
        in_specs = [per_view(a.shape) for a in args]
        kernel = later_turn
    return pl.pallas_call(
        kernel,
        out_shape=shapes,
        grid=(loads + views + folds,),
        in_specs=in_specs + filters,
        out_specs=out_specs,
        scratch_shapes=scratch,
        compiler_params=pltpu.CompilerParams(vmem_limit_bytes=VMEM),
        name="turn",
    )(*args, kf, fy, fx)


NEAR = [(-1, 0), (1, 0), (0, -1), (0, 1), (-1, -1), (1, -1), (-1, 1), (1, 1)]


def inside(grid, dy, dx):
    ny, nx = grid
    y = lax.axis_index("gy") + dy
    x = lax.axis_index("gx") + dx
    return (y >= 0) & (y < ny) & (x >= 0) & (x < nx), (y, x)


def greet(grid):
    barrier = pltpu.get_barrier_semaphore()
    for dy, dx in NEAR:
        there, where = inside(grid, dy, dx)

        @pl.when(there)
        def _():
            pl.semaphore_signal(barrier, inc=1, device_id=where, device_id_type=pl.DeviceIdType.MESH)

    ny, nx = grid
    y, x = lax.axis_index("gy"), lax.axis_index("gx")
    tall = 3 - (y == 0).astype(jnp.int32) - (y == ny - 1).astype(jnp.int32)
    broad = 3 - (x == 0).astype(jnp.int32) - (x == nx - 1).astype(jnp.int32)
    pl.semaphore_wait(barrier, tall * broad - 1)


def move(i, where, moves, send_sems, recv_sems):
    source, dest = moves[i]
    return pltpu.make_async_remote_copy(
        src_ref=source, dst_ref=dest, send_sem=send_sems.at[i], recv_sem=recv_sems.at[i],
        device_id=where, device_id_type=pl.DeviceIdType.MESH,
    )


def launch(grid, which, moves, send_sems, recv_sems):
    for i in which:
        there, where = inside(grid, *NEAR[i])

        @pl.when(there)
        def _():
            move(i, where, moves, send_sems, recv_sems).start()


def land(grid, moves, send_sems, recv_sems):
    for i, (dy, dx) in enumerate(NEAR):
        there, where = inside(grid, -dy, -dx)

        @pl.when(there)
        def _():
            move(i, where, moves, send_sems, recv_sems).wait_recv()

        @pl.when(jnp.logical_not(there))
        def _():
            dest = moves[i][1]
            dest[...] = jnp.zeros(dest.shape, dest.dtype)

    for i, (dy, dx) in enumerate(NEAR):
        there, where = inside(grid, dy, dx)

        @pl.when(there)
        def _():
            move(i, where, moves, send_sems, recv_sems).wait_send()


def widen(grid, fresh, wide_ref, left, right, rows, from_left, from_right, send_sems, recv_sems):
    planes, ext, _ = wide_ref.shape
    side = ext - 2 * PAD

    first, last = pl.ds(0, PAD), pl.ds(side - PAD, PAD)
    whole, before, after = pl.ds(0, side), pl.ds(side, PAD), pl.ds(side + PAD, PAD)
    lanes = pl.ds(0, side)
    moves = [
        (wide_ref.at[:, first, lanes], rows.at[:, pl.ds(PAD, PAD)]),
        (wide_ref.at[:, last, lanes], rows.at[:, pl.ds(0, PAD)]),
        (left, from_right.at[:, whole]),
        (right, from_left.at[:, whole]),
        (left.at[:, first], from_right.at[:, after]),
        (left.at[:, last], from_right.at[:, before]),
        (right.at[:, first], from_left.at[:, after]),
        (right.at[:, last], from_left.at[:, before]),
    ]

    def cast(z, carry):
        wide_ref[z, :side, :side] = fresh(z).astype(jnp.bfloat16)
        return carry

    lax.fori_loop(0, planes, cast, 0, unroll=4)
    launch(grid, (0, 1), moves, send_sems, recv_sems)

    def cut(p, carry):
        values = [fresh(p * 8 + k) for k in range(8)]
        left[p] = fold_lanes(values, 0).astype(jnp.bfloat16)
        right[p] = fold_lanes(values, side - PAD).astype(jnp.bfloat16)
        return carry

    lax.fori_loop(0, planes // 8, cut, 0)
    launch(grid, range(2, 8), moves, send_sems, recv_sems)
    land(grid, moves, send_sems, recv_sems)

    def paste(p, carry):
        low = from_left[p].astype(jnp.float32)
        high = from_right[p].astype(jnp.float32)
        for k in range(8):
            rim = unfold_lanes(low, k, 0) + unfold_lanes(high, k, PAD)
            wide_ref[p * 8 + k, :, side:] = rim.astype(jnp.bfloat16)
            wide_ref[p * 8 + k, side:, :side] = rows[p * 8 + k]
        return carry

    lax.fori_loop(0, planes // 8, paste, 0)


def rim_scratch(planes, side):
    ext = side + 2 * PAD
    return [
        pltpu.VMEM((planes, 2 * PAD, side), jnp.bfloat16),
        pltpu.VMEM((planes // 8, ext, side), jnp.bfloat16),
        pltpu.VMEM((planes // 8, ext, side), jnp.bfloat16),
        pltpu.SemaphoreType.DMA((8,)),
        pltpu.SemaphoreType.DMA((8,)),
    ]


def fold_scratch(planes, side):
    return [pltpu.VMEM((planes // 8, side, side), jnp.bfloat16)] * 2


def gather(grid, in_ref, ys_ref, xl_ref, xr_ref, rows, from_left, from_right, send_sems, recv_sems):
    planes, side, _ = in_ref.shape
    whole, before, after = pl.ds(0, side), pl.ds(side, PAD), pl.ds(side + PAD, PAD)
    first, second = pl.ds(0, PAD), pl.ds(PAD, PAD)
    moves = [
        (ys_ref.at[:, first], rows.at[:, second]),
        (ys_ref.at[:, second], rows.at[:, first]),
        (xl_ref.at[:, whole], from_right.at[:, whole]),
        (xr_ref.at[:, whole], from_left.at[:, whole]),
        (xl_ref.at[:, before], from_right.at[:, after]),
        (xl_ref.at[:, after], from_right.at[:, before]),
        (xr_ref.at[:, before], from_left.at[:, after]),
        (xr_ref.at[:, after], from_left.at[:, before]),
    ]
    launch(grid, range(8), moves, send_sems, recv_sems)
    land(grid, moves, send_sems, recv_sems)


def totals(z, p, k, in_ref, rows, from_left, from_right):
    side = in_ref.shape[1]
    gap = jnp.zeros((side - 2 * PAD, side), jnp.float32)
    edge = rows[z].astype(jnp.float32)

    def rim(held, start):
        held = held.astype(jnp.float32)
        body = held[:side] + jnp.concatenate([held[side : side + PAD], gap, held[side + PAD :]], axis=0)
        return unfold_lanes(body, k, start)

    total = in_ref[z] + jnp.concatenate([edge[:PAD], gap, edge[PAD:]], axis=0)
    return total + rim(from_left[p], 0) + rim(from_right[p], side - PAD)


def first_kernel(grid, est_ref, wide_ref, left, right, *rim):
    greet(grid)
    widen(grid, lambda z: est_ref[z], wide_ref, left, right, *rim)


def between_kernel(grid, views, est_ref, in_ref, ys_ref, xl_ref, xr_ref, new_ref, wide_ref, *scratch):
    greet(grid)
    rim, (left, right), again = scratch[:5], scratch[5:7], scratch[7:]
    gather(grid, in_ref, ys_ref, xl_ref, xr_ref, *rim)

    def update(p, carry):
        for k in range(8):
            z = p * 8 + k
            new_ref[z] = est_ref[z] * totals(z, p, k, in_ref, *rim[:3]) / views
        return carry

    lax.fori_loop(0, est_ref.shape[0] // 8, update, 0)
    widen(grid, lambda z: new_ref[z], wide_ref, left, right, *again)


def last_kernel(grid, views, est_ref, in_ref, ys_ref, xl_ref, xr_ref, out_ref, *rim):
    greet(grid)
    gather(grid, in_ref, ys_ref, xl_ref, xr_ref, *rim)

    def update(p, carry):
        for k in range(8):
            z = p * 8 + k
            out_ref[z] = est_ref[z] * totals(z, p, k, in_ref, *rim[:3]) / views
        return carry

    lax.fori_loop(0, in_ref.shape[0] // 8, update, 0)


def rim_call(kernel, name, number, shapes, scratch, args):
    held = pl.BlockSpec(memory_space=pltpu.VMEM)
    return pl.pallas_call(
        kernel,
        out_shape=shapes,
        in_specs=[held] * len(args),
        out_specs=[held] * len(shapes),
        scratch_shapes=scratch,
        compiler_params=pltpu.CompilerParams(
            vmem_limit_bytes=VMEM, collective_id=number, has_side_effects=True
        ),
        name=name,
    )(*args)


def local(tiles, tile_dest, tile_slot, psf, estimate):
    devices = lax.axis_size("gy") * lax.axis_size("gx")
    holding, side, _ = tiles.shape
    slot_count = 2 * ((holding + devices - 1) // devices)
    views, _, taps = psf.shape
    planes = estimate.shape[0]
    target = tile_dest[:, 0]
    earlier = (target[None, :] == target[:, None]) & (
        jnp.arange(holding)[None, :] < jnp.arange(holding)[:, None]
    )
    rank = jnp.sum(earlier.astype(jnp.int32), axis=1)
    where_to = target * slot_count + rank
    placing = where_to[None, :] == jnp.arange(devices * slot_count)[:, None]
    pick = jnp.sum(jnp.where(placing, jnp.arange(holding, dtype=jnp.int32)[None, :], 0), axis=1)
    labels = jnp.sum(jnp.where(placing, tile_slot[None, :] + 1, 0), axis=1) - 1
    packed = pack(pick, tiles)
    exchange = functools.partial(
        lax.all_to_all, axis_name=("gy", "gx"), split_axis=0, concat_axis=0, tiled=True
    )
    got_labels = exchange(labels.reshape(devices, slot_count)).reshape(-1)
    grid = (lax.axis_size("gy"), lax.axis_size("gx"))
    volume = jax.ShapeDtypeStruct(estimate.shape, jnp.float32)
    framed = jax.ShapeDtypeStruct((planes, side + 2 * PAD, 2 * side), jnp.bfloat16)
    rim, folds = rim_scratch(planes, side), fold_scratch(planes, side)
    (wide,) = rim_call(functools.partial(first_kernel, grid), "rim_first", 0, [framed], folds + rim, [estimate])
    packed, psf, got_labels, wide = lax.optimization_barrier((packed, psf, got_labels, wide))
    got_tiles = exchange(packed.reshape(devices, slot_count, side, side)).reshape(-1, side, side)

    kernel = (psf / jnp.sum(psf, axis=2, keepdims=True)).astype(jnp.bfloat16).astype(jnp.float32)
    bx, by, kz, kf, fy, fx = bands(kernel.reshape(views * 3, taps), planes, side)

    sorting = got_labels[None, :] == jnp.arange(views * planes)[:, None]
    counted = jnp.sum(sorting.astype(jnp.float32), axis=1).reshape(views, planes)
    count = jnp.broadcast_to(counted[:, :, None], (views, planes, side))
    seen = None
    for repeat_index in range(ITERS):
        along = sides(wide, bx, by)
        if seen is None:
            weight = weigh(along, count, kz)
            *parts, seen = turn([got_labels, got_tiles, weight], kf, fy, fx, got_tiles.shape[0] // 32)
        else:
            parts = turn([along, seen, count, kz], kf, fy, fx)
        if repeat_index + 1 < ITERS:
            estimate, wide = rim_call(
                functools.partial(between_kernel, grid, views), "rim_between", 1,
                [volume, framed], rim + folds + rim, [estimate, *parts],
            )
        else:
            (estimate,) = rim_call(
                functools.partial(last_kernel, grid, views), "rim_last", 2, [volume], rim, [estimate, *parts]
            )
    return estimate


def solution(mesh):
    placed = (
        P(("gy", "gx"), None, None),
        P(("gy", "gx"), None),
        P(("gy", "gx")),
        P(),
        P(None, "gy", "gx"),
    )
    return jax.shard_map(
        local, mesh=mesh, in_specs=placed, out_specs=P(None, "gy", "gx"), check_vma=False
    )
```
